256 devices in a mesh: req: 32 (over x, z), head: 8 (over y, core).
Axes of the slice: x: 4, y: 4, z: 8, core: 2. Of those that a mesh axis runs over, the one named last changes fastest.
Arguments:
- states: float32 [256, 64, 64, 128], P('req', 'head'), may hold values from -1.75 to 1.75
- ssm_x: bfloat16 [3, 256, 4096], P(None, 'req', 'head'), may hold values from -6 to 6
- gate_z: bfloat16 [3, 256, 4096], P(None, 'req', 'head'), may hold values from -6 to 6
- ssm_b: bfloat16 [3, 256, 1024], P(None, 'req', 'head'), may hold values from -3 to 3
- ssm_c: bfloat16 [3, 256, 1024], P(None, 'req', 'head'), may hold values from -3 to 3
- dt_raw: float32 [3, 256, 64], P(None, 'req', 'head'), may hold values from -6 to 6
- decay_rate: float32 [64], P('head'), may hold values from 0.05 to 2
- skip_gain: float32 [64], P('head'), may hold values from 0.5 to 2
- ssm_gain: float32 [4096], P('head'), may hold values from 0.5 to 1.5
- out_weight: bfloat16 [4096, 4096], P('head'), may hold values from -0.09375 to 0.09375
- residual: bfloat16 [3, 256, 4096], P(None, 'req'), may hold values from -32 to 32
- ffn_gain: float32 [4096], P('head'), may hold values from 0.5 to 1.5
- route_ids: int32 [3, 256, 8], P(None, 'req'), may hold values from 0 to 63, all different within a row; in each aligned block of 8 rows (0 to 7, 8 to 15, ..., all dimensions but the last counted through in order) at most 2 rows name the same one
- route_weights: float32 [3, 256, 8], P(None, 'req'), may hold values from 0.02 to 0.25
- gate_weight: bfloat16 [64, 4096, 1024], P('req', 'head'), may hold values from -0.09375 to 0.09375
- up_weight: bfloat16 [64, 4096, 1024], P('req', 'head'), may hold values from -0.09375 to 0.09375
- down_weight: bfloat16 [64, 1024, 4096], P('req', None, 'head'), may hold values from -0.1875 to 0.1875
- dest: int32 [2, 256], replicated, may hold values from 0 to 255, as said below
Outputs:
- mixed: bfloat16 [3, 256, 4096], P(None, 'req', 'head')
- final_states: float32 [256, 64, 64, 128], P('req', 'head')
The draws below stay inside these ranges and needn't reach their ends.
Inputs may be any that keep to these rules, and one draw needn't show every extreme that they name: `route_ids`: in each step the 8 slots of one device name each expert at most 2 times, and each slot names 8 different experts. Each row is a permutation of the 256 slots: the request in slot g sits in slot dest[w, g] after wave w + 1. In each wave every device's block of 8 slots sends exactly 7 requests, to 7 different other devices, and takes the 7 arriving requests into the slots it vacated; all other requests stay in their slots.
All inputs are finite; a program needn't handle non-finite values.
Results may differ from the reference program's by a relative error of at most 0.013.
Values may be sent and summed in bfloat16 or wider, within the bound.
No kernel may reach another device: no remote copies, remote signals or barrier semaphores. Data moves between devices by JAX's collectives and lax.ppermute only.
A program may use at most 128 MiB of HBM per device.

```python
import math
import jax
import jax.numpy as jnp
import numpy as np
from jax import lax

SLOTS = 8
D = 4096
H = 64
HSIZE = 64
NSTATE = 128
NGROUPS = 8
EXPERTS = 64
FFE = 1024
TOP = 8
STEPS = 3
WAVES = 2
CAP = 2
REQUESTS = 256


def draw_residual(key, part):
    key = jax.random.fold_in(key, 5)
    row_key, column_key, value_key = jax.random.split(key, 3)
    row_scale = jnp.exp(jax.random.uniform(row_key, (STEPS, REQUESTS, 1), jnp.float32, -1.15, 1.15))
    column_scale = jnp.exp(jax.random.uniform(column_key, (1, 1, D), jnp.float32, -1.15, 1.15))
    values = jnp.clip(jax.random.normal(value_key, (STEPS, REQUESTS, D), jnp.float32), -6.0, 6.0)
    return (values * row_scale * column_scale * 0.5).astype(jnp.bfloat16)


def slot_shuffle(sub_key):
    return jax.random.permutation(sub_key, SLOTS)


def draw_dest(key, part):
    key = jax.random.fold_in(key, 7)
    owners = REQUESTS // SLOTS
    move_count = min(SLOTS - 1, owners - 1)
    plans = []
    for wave_index in range(WAVES):
        wave_key = jax.random.fold_in(key, wave_index)
        order_key, shift_key, slot_key = jax.random.split(wave_key, 3)
        device_order = jax.random.permutation(order_key, owners).astype(jnp.int32)
        inverse_order = jnp.zeros((owners,), jnp.int32).at[device_order].set(jnp.arange(owners, dtype=jnp.int32))
        shifts = (1 + jax.random.permutation(shift_key, owners - 1)[:move_count]).astype(jnp.int32)
        slot_order = jax.vmap(slot_shuffle)(jax.random.split(slot_key, owners)).astype(jnp.int32)
        senders = jnp.arange(owners, dtype=jnp.int32)[:, None]
        rounds = jnp.arange(move_count, dtype=jnp.int32)[None, :]
        receivers = device_order[(inverse_order[senders] + shifts[rounds]) % owners]
        sources = senders * SLOTS + slot_order[senders, rounds]
        targets = receivers * SLOTS + slot_order[receivers, rounds]
        plan = jnp.arange(REQUESTS, dtype=jnp.int32).at[sources.reshape(-1)].set(targets.reshape(-1))
        plans.append(plan)
    return jnp.stack(plans).astype(jnp.int32)


def levels(own_key, extent, shards, smallest, top_value):
    loudness = 1.0
    for position, blocks in shards:
        heights = jax.random.uniform(jax.random.fold_in(jax.random.fold_in(own_key, 6), position), (blocks,), jnp.float32, smallest / len(shards), top_value / len(shards))
        loudness = loudness * jnp.repeat(jnp.exp(heights), extent[position] // blocks).reshape((-1,) + (1,) * (len(extent) - 1 - position))
    return loudness


def deal_out(stream_key, own, number, rows, amount, top, bound, lean):
    sequence = jax.random.permutation(stream_key, amount)
    crowded, usual = shares(amount, rows * top, bound, lean, True), shares(amount, rows * top, bound, lean, False)
    places = jnp.arange(amount)

    def named(tallies, offset_by):
        used = int((tallies > 0).sum())
        fixed = max(1, used // 4)
        shifted = fixed + (places - fixed + offset_by * (used - fixed)) % max(1, amount - fixed)
        return jnp.zeros((amount,), jnp.int32).at[sequence[jnp.where(places < fixed, places, shifted)]].set(jnp.asarray(tallies, jnp.int32))

    tallies = jnp.where(number % 4 == 0, named(crowded, number // 4), named(usual, number - number // 4 - 1))
    mixed = jax.random.permutation(jax.random.fold_in(own, 3), amount)
    source_of, receiver = mixed[0:amount // 2 * 2:2], mixed[1:amount // 2 * 2:2]
    slack = jnp.minimum(tallies[source_of] - 1, bound - tallies[receiver]) // 2
    slack = jnp.where((source_of == sequence[0]) | (receiver == sequence[0]) | (tallies[receiver] == 0), 0, jnp.maximum(slack, 0))
    shifted = jax.random.randint(jax.random.fold_in(own, 4), (amount // 2,), 0, 1 << 20) % (slack + 1)
    tallies = tallies.at[source_of].add(-shifted).at[receiver].add(shifted)
    members = jnp.searchsorted(jnp.cumsum(tallies), jnp.arange(rows * top), side="right").astype(jnp.int32)
    grid = members.reshape(top, rows).T
    grid = grid[jax.random.permutation(jax.random.fold_in(own, 1), rows)]
    offset_by = jax.random.randint(jax.random.fold_in(own, 2), (rows, 1), 0, top)
    return jnp.take_along_axis(grid, (jnp.arange(top)[None, :] + offset_by) % top, axis=1)


def shares(number_of, total, bound, slope, full):
    portions = [(1 << 20) // math.isqrt(standing ** slope) + 1 for standing in range(1, number_of + 1)]
    largest = bound if full else min(bound, max(-(-total // number_of), total * portions[0] // sum(portions)))
    least = 1 if total - largest >= number_of - 1 else 0
    holding, rest = [largest] + [least] * (number_of - 1), total - largest - least * (number_of - 1)
    while rest > 0:
        candidates = [i for i in range(1, number_of) if holding[i] < largest] or [i for i in range(1, number_of) if holding[i] < bound]
        pool, remaining = sum([portions[i] for i in candidates]), rest
        for i in candidates:
            more = min(bound - holding[i], max(1, remaining * portions[i] // pool), rest)
            holding[i] = holding[i] + more
            rest = rest - more
    return np.array(holding)


def gaussian(key, shape, width, bound, shards=(), held_as=jnp.bfloat16):
    values = width * jax.random.normal(key, shape, jnp.float32)
    if shards:
        values = values * levels(key, shape, shards, -0.22, 0.18)
    return jnp.clip(values, -bound, bound).astype(held_as)


def setup_inputs(seed: int = 0) -> dict:
    streams_of = jax.random.split(jax.random.key(seed), 19)
    states = gaussian(streams_of[0], (REQUESTS, H, HSIZE, NSTATE), 0.3, 1.75, ((0, 32), (1, 8)), jnp.float32)
    ssm_x = gaussian(streams_of[1], (STEPS, REQUESTS, H * HSIZE), 1.0, 6.0, ((1, 32), (2, 8)))
    gate_z = gaussian(streams_of[2], (STEPS, REQUESTS, H * HSIZE), 1.0, 6.0, ((1, 32), (2, 8)))
    ssm_b = gaussian(streams_of[3], (STEPS, REQUESTS, NGROUPS * NSTATE), 0.5, 3.0, ((1, 32), (2, 8)))
    ssm_c = gaussian(streams_of[4], (STEPS, REQUESTS, NGROUPS * NSTATE), 0.5, 3.0, ((1, 32), (2, 8)))
    dt_raw = gaussian(streams_of[5], (STEPS, REQUESTS, H), 1.0, 6.0, ((1, 32), (2, 8)), jnp.float32)
    decay_rate = jnp.clip(jnp.exp(math.log(2.0) - 3.6888794 * jax.random.uniform(streams_of[6], (H,), jnp.float32) ** levels(streams_of[6], (H,), ((0, 8),), -0.2, 0.2)), 0.05, 2.0)
    skip_gain = jnp.clip(0.5 + 1.5 * jax.random.uniform(streams_of[7], (H,), jnp.float32) ** levels(streams_of[7], (H,), ((0, 8),), -0.2, 0.2), 0.5, 2.0)
    ssm_gain = jnp.clip(1.0 + 0.1 * jax.random.normal(streams_of[8], (H * HSIZE,), jnp.float32), 0.5, 1.5)
    out_weight = gaussian(streams_of[9], (H * HSIZE, D), (H * HSIZE) ** -0.5, 0.09375, ((0, 8),))
    residual = draw_residual(jax.random.fold_in(streams_of[18], 71), 0)
    ffn_gain = jnp.clip(1.0 + 0.1 * jax.random.normal(streams_of[11], (D,), jnp.float32), 0.5, 1.5)
    route_ids_keys = jax.random.split(jax.random.fold_in(streams_of[12], 1), STEPS * REQUESTS // SLOTS)
    route_ids_turns = jax.random.permutation(jax.random.fold_in(streams_of[12], 3), STEPS * REQUESTS // SLOTS)
    route_ids = jax.vmap(lambda own, number: deal_out(jax.random.fold_in(streams_of[12], 2), own, number, SLOTS, EXPERTS, TOP, CAP, 1))(route_ids_keys, route_ids_turns).reshape((STEPS, REQUESTS, TOP))
    route_weights = jnp.clip(0.02 + 0.23 * jax.random.uniform(streams_of[13], (STEPS, REQUESTS, TOP), jnp.float32) ** levels(streams_of[13], (STEPS, REQUESTS, TOP), ((1, 32),), -0.2, 0.2), 0.02, 0.25)
    gate_weight = gaussian(streams_of[14], (EXPERTS, D, FFE), D ** -0.5, 0.09375, ((0, 32), (1, 8)))
    up_weight = gaussian(streams_of[15], (EXPERTS, D, FFE), D ** -0.5, 0.09375, ((0, 32), (1, 8)))
    down_weight = gaussian(streams_of[16], (EXPERTS, FFE, D), FFE ** -0.5, 0.1875, ((0, 32), (2, 8)))
    dest = draw_dest(jax.random.fold_in(streams_of[18], 71), 0)
    return dict(states=states, ssm_x=ssm_x, gate_z=gate_z, ssm_b=ssm_b, ssm_c=ssm_c, dt_raw=dt_raw, decay_rate=decay_rate, skip_gain=skip_gain, ssm_gain=ssm_gain, out_weight=out_weight, residual=residual, ffn_gain=ffn_gain, route_ids=route_ids, route_weights=route_weights, gate_weight=gate_weight, up_weight=up_weight, down_weight=down_weight, dest=dest)


NORM_EPS = 1e-05

def expand_groups(packed_rows):
    grouped = packed_rows.astype(jnp.float32).reshape(packed_rows.shape[0], NGROUPS, NSTATE)
    return jnp.repeat(grouped, H // NGROUPS, axis=1)

def advance(prior, inputs_x, raw_dt, decay_rates, b_state):
    step_size = jax.nn.softplus(raw_dt)
    retained = jnp.exp(-decay_rates[None, :] * step_size)
    return retained[:, :, None, None] * prior + (step_size[:, :, None] * inputs_x)[:, :, :, None] * b_state[:, :, None, :]

def mixture(row_block, route_rows, row_weights, gate_weight, up_weight, down_weight):
    flat_ids = route_rows.reshape(-1).astype(jnp.int32)
    flat_weights = row_weights.reshape(-1)
    most_rows = REQUESTS // SLOTS * CAP

    def one_expert(running, expert):
        chosen = flat_ids == expert
        picked = jnp.nonzero(chosen, size=most_rows, fill_value=0)[0]
        live_rows = (jnp.arange(most_rows) < jnp.sum(chosen)).astype(jnp.float32)
        token_rows = picked // TOP
        inputs = row_block[token_rows]
        gate_pre = jnp.dot(inputs, gate_weight[expert], preferred_element_type=jnp.float32)
        up_pre = jnp.dot(inputs, up_weight[expert], preferred_element_type=jnp.float32)
        hidden = (jax.nn.silu(gate_pre) * up_pre).astype(jnp.bfloat16)
        result = jnp.dot(hidden, down_weight[expert], preferred_element_type=jnp.float32).astype(jnp.bfloat16)
        row_scale = flat_weights[picked] * live_rows
        return (running.at[token_rows].add(row_scale[:, None] * result.astype(jnp.float32)), None)
    start_sum = jnp.zeros((row_block.shape[0], D), jnp.float32)
    return lax.scan(one_expert, start_sum, jnp.arange(EXPERTS, dtype=jnp.int32))[0]

def reference(states, ssm_x, gate_z, ssm_b, ssm_c, dt_raw, decay_rate, skip_gain, ssm_gain, out_weight, residual, ffn_gain, route_ids, route_weights, gate_weight, up_weight, down_weight, dest):
    ssm_state = states
    outputs = []
    for step_index in range(STEPS):
        if step_index > 0:
            ssm_state = jnp.zeros_like(ssm_state).at[dest[step_index - 1]].set(ssm_state)
        inputs_x = ssm_x[step_index].astype(jnp.float32).reshape(REQUESTS, H, HSIZE)
        ssm_state = advance(ssm_state, inputs_x, dt_raw[step_index], decay_rate, expand_groups(ssm_b[step_index]))
        y_out = jnp.einsum('shpn,shn->shp', ssm_state, expand_groups(ssm_c[step_index]), precision=lax.Precision.HIGHEST) + skip_gain[None, :, None] * inputs_x
        gate_rows = gate_z[step_index].astype(jnp.float32).reshape(REQUESTS, H, HSIZE)
        gated_out = y_out * jax.nn.silu(gate_rows)
        grouped = gated_out.reshape(REQUESTS, NGROUPS, H // NGROUPS * HSIZE)
        normed = grouped * lax.rsqrt(lax.optimization_barrier(jnp.mean(grouped * grouped, axis=-1, keepdims=True)) + NORM_EPS)
        mamba_out = (normed.reshape(REQUESTS, H * HSIZE) * ssm_gain).astype(jnp.bfloat16)
        projected = jnp.dot(mamba_out, out_weight, preferred_element_type=jnp.float32)
        stream = (residual[step_index].astype(jnp.float32) + projected).astype(jnp.bfloat16)
        stream_wide = stream.astype(jnp.float32)
        inverse = lax.rsqrt(lax.optimization_barrier(jnp.mean(stream_wide * stream_wide, axis=-1, keepdims=True)) + NORM_EPS)
        normed_rows = (stream_wide * inverse * ffn_gain).astype(jnp.bfloat16)
        expert_mix = mixture(normed_rows, route_ids[step_index], route_weights[step_index], gate_weight, up_weight, down_weight)
        outputs.append((stream_wide + expert_mix).astype(jnp.bfloat16))
    return (jnp.stack(outputs), ssm_state)
```

```python
import jax
import jax.numpy as jnp
from jax import lax
from jax.experimental import pallas as pl
from jax.experimental.pallas import tpu as pltpu
from jax.sharding import PartitionSpec as P

NSTATE = 128
EXPERTS = 64
STEPS = 3
CAP = 2
OWNERS = 32
SLOTS = 8
REQUESTS = OWNERS * SLOTS
HEADS = 8
HSIZE = 64
WIDTH = 512
GROUP_HEADS = 8
NORM_EPS = 1e-05
F32 = jnp.float32
BF16 = jnp.bfloat16
VMEM = pltpu.VMEM
SMEM = pltpu.SMEM


def split_pair(value):
    high = value.astype(BF16)
    low = (value - high.astype(F32)).astype(BF16)
    return high, low


def contract(a, b, dims):
    return lax.dot_general(a, b, (dims, ((), ())), preferred_element_type=F32)


def plan_kernel(dest_ref, table_ref):
    size = (REQUESTS, REQUESTS)
    row_id = lax.broadcasted_iota(jnp.int32, size, 1)
    col_id = lax.broadcasted_iota(jnp.int32, size, 0)
    first_row = jnp.broadcast_to(dest_ref[0:1, :], size)
    second_row = jnp.broadcast_to(dest_ref[1:2, :], size)
    first_col = jnp.transpose(first_row)
    hop = (first_col == row_id).astype(BF16)
    second_col = jnp.transpose(second_row).astype(F32).astype(BF16)
    final_col = contract(hop, second_col, ((1,), (0,))).astype(jnp.int32)
    final_row = jnp.transpose(final_col)
    differs = row_id != col_id
    color_col = jnp.zeros(size, jnp.int32)
    color_row = color_col
    for level in (1, 2, 3):
        alike = (color_col == color_row) & differs
        source = jnp.where(((row_id >> level) == (col_id >> level)) & alike, 1.0, 0.0).astype(BF16)
        target = jnp.where(((final_row >> level) == (final_col >> level)) & alike, 1.0, 0.0).astype(BF16)
        power = contract(source, target, ((1,), (0,))).astype(BF16)
        least = col_id.astype(F32)
        for turn in range(7):
            ahead = contract(power, least.astype(BF16), ((1,), (0,)))
            least = jnp.minimum(least, ahead)
            if turn < 6:
                power = contract(power, power, ((1,), (0,))).astype(BF16)
        other = contract(source, least.astype(BF16), ((1,), (0,)))
        bit = jnp.where(least > other, 1, 0)
        color_col = color_col * 2 + bit
        color_row = jnp.transpose(color_col)

    def lookup(key, value):
        return jnp.sum(jnp.where(key == row_id, value, 0), axis=0, keepdims=True)

    table_ref[...] = jnp.zeros_like(table_ref)
    table_ref[0:1, :] = lookup((col_id & -8) + color_col, col_id & 7)
    table_ref[1:2, :] = lookup(color_col * OWNERS + (final_col >> 3), col_id >> 3)
    table_ref[2:3, :] = lookup(final_col, color_col)


def routing_tables(dest):
    return pl.pallas_call(
        plan_kernel,
        out_shape=jax.ShapeDtypeStruct((8, REQUESTS), jnp.int32),
        in_specs=[pl.BlockSpec(memory_space=VMEM)],
        out_specs=pl.BlockSpec(memory_space=VMEM),
        compiler_params=pltpu.CompilerParams(vmem_limit_bytes=16 * 2**20),
        cost_estimate=pl.CostEstimate(flops=3 * 16 * 2 * 256**3, bytes_accessed=16384, transcendentals=0),
        name="plan_states",
    )(dest)


def mamba_kernel(
    state_ref, x_ref, z_ref, b_ref, c_ref, dt_ref, decay_ref, skip_ref, gain_ref, weight_ref,
    part_ref, outer_ref, keep_ref, read_ref, rows_ref,
):
    head_of = lax.broadcasted_iota(jnp.int32, (HEADS, WIDTH), 1) // HSIZE
    spread = (head_of == lax.broadcasted_iota(jnp.int32, (HEADS, WIDTH), 0)).astype(F32)

    def widen(value):
        return lax.dot_general(
            value, spread, (((1,), (0,)), ((), ())),
            precision=lax.Precision.HIGHEST, preferred_element_type=F32,
        )

    for slot in range(SLOTS):
        high, low = split_pair(state_ref[slot])
        c_rows = c_ref[slot].astype(BF16)
        read_ref[slot] = contract(c_rows, high, ((1,), (1,))) + contract(c_rows, low, ((1,), (1,)))
    skip = widen(jnp.broadcast_to(skip_ref[...], (HEADS, HEADS)))
    inputs, kept, steps_b, steps_c = [], [], [], []
    for step in range(STEPS):
        raw = dt_ref[step]
        step_size = jnp.maximum(raw, 0.0) + jnp.log1p(jnp.exp(-jnp.abs(raw)))
        kept.append(widen(jnp.exp(-decay_ref[...] * step_size)))
        inputs.append(widen(step_size) * x_ref[step].astype(F32))
        steps_b.append(b_ref[:, step, :])
        steps_c.append(c_ref[:, step, :])
    for step in range(STEPS):
        total = read_ref[:, step, :] * kept[0]
        for earlier in range(step + 1):
            if earlier > 0:
                total = total * kept[earlier]
            match = jnp.sum(steps_b[earlier] * steps_c[step], axis=1, keepdims=True)
            total = total + inputs[earlier] * match
        y_out = total + skip * x_ref[step].astype(F32)
        gate = z_ref[step].astype(F32)
        gated = y_out * (gate / (1.0 + jnp.exp(-gate)))
        scale = lax.rsqrt(jnp.mean(gated * gated, axis=1, keepdims=True) + NORM_EPS)
        rows_ref[step * SLOTS : (step + 1) * SLOTS, :] = gated * scale * gain_ref[...]
    rows = rows_ref[...].astype(BF16)
    for block in range(HEADS):
        columns = slice(block * WIDTH, (block + 1) * WIDTH)
        part_ref[block] = contract(rows, weight_ref[:, columns], ((1,), (0,))).astype(BF16)
    late = kept[2]
    factors = [inputs[0] * (kept[1] * late), inputs[1] * late, inputs[2]]
    outer_ref[...] = jnp.zeros_like(outer_ref)
    keep_ref[...] = jnp.zeros_like(keep_ref)
    for step in range(STEPS):
        outer_ref[:, step, :] = factors[step]
    keep_ref[:, 0, :] = kept[0] * (kept[1] * late)


def mamba(state, x, z, b, c, dt, decay, skip, gain, weight):
    vmem = pl.BlockSpec(memory_space=VMEM)
    return pl.pallas_call(
        mamba_kernel,
        out_shape=(
            jax.ShapeDtypeStruct((HEADS, STEPS * SLOTS, WIDTH), BF16),
            jax.ShapeDtypeStruct((SLOTS, 8, WIDTH), F32),
            jax.ShapeDtypeStruct((SLOTS, 8, WIDTH), F32),
        ),
        in_specs=[vmem] * 10,
        out_specs=(vmem, vmem, vmem),
        scratch_shapes=[pltpu.VMEM((SLOTS, 8, WIDTH), F32), pltpu.VMEM((STEPS * SLOTS, WIDTH), F32)],
        compiler_params=pltpu.CompilerParams(vmem_limit_bytes=24 * 2**20),
        cost_estimate=pl.CostEstimate(flops=2 * 24 * 512 * 4096, bytes_accessed=6 * 2**20, transcendentals=0),
        name="mamba_steps",
    )(state, x, z, b, c, dt, decay, skip, gain, weight)


def update_kernel(order_ref, state_ref, outer_ref, keep_ref, b_ref, out_ref):
    ones = jnp.ones((8, NSTATE), BF16)
    b_rows = b_ref[0].astype(BF16)
    outer_high, outer_low = split_pair(outer_ref[0])
    keep_high, keep_low = split_pair(keep_ref[0])
    along = ((0,), (0,))
    keep = contract(keep_high, ones, along) + contract(keep_low, ones, along)
    added = contract(outer_high, b_rows, along) + contract(outer_low, b_rows, along)
    out_ref[0] = (keep * state_ref[0] + added).astype(BF16)


def update_states(order, state, outer, keep, b):
    def picked(step, order_ref):
        return (order_ref[step], 0, 0)

    return pl.pallas_call(
        update_kernel,
        out_shape=jax.ShapeDtypeStruct((SLOTS, HEADS * HSIZE, NSTATE), BF16),
        grid_spec=pltpu.PrefetchScalarGridSpec(
            num_scalar_prefetch=1,
            grid=(SLOTS,),
            in_specs=[
                pl.BlockSpec((1, HEADS * HSIZE, NSTATE), picked),
                pl.BlockSpec((1, 8, WIDTH), picked),
                pl.BlockSpec((1, 8, WIDTH), picked),
                pl.BlockSpec((1, 8, NSTATE), picked),
            ],
            out_specs=pl.BlockSpec((1, HEADS * HSIZE, NSTATE), lambda step, order_ref: (step, 0, 0)),
        ),
        compiler_params=pltpu.CompilerParams(vmem_limit_bytes=16 * 2**20),
        cost_estimate=pl.CostEstimate(flops=2 * 32 * 512 * 1024, bytes_accessed=3 * 2**20, transcendentals=0),
        name="update_states",
    )(order, state, outer, keep, b)


def reorder_kernel(order_ref, in_ref, out_ref, sems):
    copies = [
        pltpu.make_async_copy(in_ref.at[order_ref[block]], out_ref.at[block], sems.at[block])
        for block in range(OWNERS)
    ]
    for copy in copies:
        copy.start()
    for copy in copies:
        copy.wait()


def reorder_states(order, pieces):
    return pl.pallas_call(
        reorder_kernel,
        out_shape=jax.ShapeDtypeStruct(pieces.shape, pieces.dtype),
        in_specs=[pl.BlockSpec(memory_space=SMEM), pl.BlockSpec(memory_space=pl.ANY)],
        out_specs=pl.BlockSpec(memory_space=pl.ANY),
        scratch_shapes=[pltpu.SemaphoreType.DMA((OWNERS,))],
        cost_estimate=pl.CostEstimate(flops=0, bytes_accessed=2 * 2**20, transcendentals=0),
        name="reorder_states",
    )(order, pieces)


def place_kernel(order_ref, in_ref, out_ref):
    out_ref[0] = in_ref[0].astype(F32)


def place_states(order, items):
    return pl.pallas_call(
        place_kernel,
        out_shape=jax.ShapeDtypeStruct(items.shape, F32),
        grid_spec=pltpu.PrefetchScalarGridSpec(
            num_scalar_prefetch=1,
            grid=(SLOTS,),
            in_specs=[pl.BlockSpec((1, HEADS * HSIZE, NSTATE), lambda step, order_ref: (order_ref[step], 0, 0))],
            out_specs=pl.BlockSpec((1, HEADS * HSIZE, NSTATE), lambda step, order_ref: (step, 0, 0)),
        ),
        cost_estimate=pl.CostEstimate(flops=0, bytes_accessed=3 * 2**20, transcendentals=0),
        name="place_states",
    )(order, items)


def expand_kernel(pick_ref, stream_ref, gain_ref, gate_ref, up_ref, out_ref):
    half = pick_ref.shape[0] // 2
    for expert in range(2):
        rows = slice(expert * half, (expert + 1) * half)
        picked = contract(pick_ref[rows, :], stream_ref[...], ((1,), (0,)))
        square = jnp.sum(picked * picked, axis=1, keepdims=True)
        high, low = split_pair(square)
        lane = lax.broadcasted_iota(jnp.int32, (half, 128), 1)
        high_wide = jnp.broadcast_to(high.astype(F32), (half, 128))
        low_wide = jnp.broadcast_to(low.astype(F32), (half, 128))
        pair = jnp.where(lane == 0, high_wide, jnp.where(lane == 1, low_wide, 0.0))
        scaled = (picked * gain_ref[...]).astype(BF16)
        out_ref[rows, 0:1024] = contract(scaled, gate_ref[expert], ((1,), (0,))).astype(BF16)
        out_ref[rows, 1024:2048] = contract(scaled, up_ref[expert], ((1,), (0,))).astype(BF16)
        out_ref[rows, 2048:2176] = pair.astype(BF16)


def expand(pick, stream, gain, gate_weight, up_weight):
    vmem = pl.BlockSpec(memory_space=VMEM)
    return pl.pallas_call(
        expand_kernel,
        out_shape=jax.ShapeDtypeStruct((pick.shape[0], 2176), BF16),
        in_specs=[vmem] * 5,
        out_specs=vmem,
        compiler_params=pltpu.CompilerParams(vmem_limit_bytes=32 * 2**20),
        cost_estimate=pl.CostEstimate(flops=2 * 384 * 512 * (2048 + 768), bytes_accessed=8 * 2**20, transcendentals=0),
        name="expand_experts",
    )(pick, stream, gain, gate_weight, up_weight)


def hidden_kernel(parts_ref, out_ref):
    total = parts_ref[0].astype(F32)
    for block in range(1, HEADS):
        total = total + parts_ref[block].astype(F32)
    square = jnp.sum(total[:, 2048:2176], axis=1, keepdims=True)
    inverse = lax.rsqrt(square * (1.0 / (HEADS * WIDTH)) + NORM_EPS)
    gate = total[:, 0:1024] * inverse
    up = total[:, 1024:2048] * inverse
    out_ref[...] = (gate / (1.0 + jnp.exp(-gate)) * up).astype(BF16)


def hidden_units(parts):
    vmem = pl.BlockSpec(memory_space=VMEM)
    return pl.pallas_call(
        hidden_kernel,
        out_shape=jax.ShapeDtypeStruct((parts.shape[1], 1024), BF16),
        in_specs=[vmem],
        out_specs=vmem,
        compiler_params=pltpu.CompilerParams(vmem_limit_bytes=16 * 2**20),
        cost_estimate=pl.CostEstimate(flops=0, bytes_accessed=2 * 2**20, transcendentals=0),
        name="hidden_units",
    )(parts)


def one_hot(index, size):
    return (index[:, None] == lax.iota(jnp.int32, size)[None, :]).astype(BF16)


def select(index, rows):
    return jnp.dot(one_hot(index, rows.shape[0]), rows, preferred_element_type=F32).astype(BF16)


def lookup(index, values):
    match = index[:, None] == lax.iota(jnp.int32, values.shape[0])[None, :]
    return jnp.sum(jnp.where(match, values[None, :], 0), axis=1)


def find(index, values):
    match = index[:, None] == values[None, :]
    return jnp.sum(jnp.where(match, lax.iota(jnp.int32, values.shape[0])[None, :], 0), axis=1)


def shards(
    states, ssm_x, gate_z, ssm_b, ssm_c, dt_raw, decay_rate, skip_gain, ssm_gain, out_weight,
    residual, ffn_gain, route_ids, route_weights, gate_weight, up_weight, down_weight, dest,
):
    me = lax.axis_index("req")
    column = lax.axis_index("head")
    own = me * SLOTS + lax.iota(jnp.int32, SLOTS)
    first_dest, second_dest = dest[0], dest[1]

    back_one = find(own, first_dest)
    back_two = find(find(own, second_dest), first_dest)
    next_one = lookup(own, first_dest)
    next_two = lookup(next_one, second_dest)

    tables = routing_tables(dest)

    own_residual = lax.dynamic_slice_in_dim(residual, column * WIDTH, WIDTH, 2)
    dt_high = lax.reduce_precision(dt_raw, 8, 7)
    dt_rest = dt_raw - dt_high
    dt_mid = lax.reduce_precision(dt_rest, 8, 7)
    dt_pieces = jnp.concatenate([dt_high, dt_mid, dt_rest - dt_mid], axis=2).astype(BF16)
    ids_wide = jnp.transpose(route_ids, (1, 0, 2)).reshape(SLOTS, STEPS * 8).astype(BF16)

    def pack(step):
        return jnp.concatenate(
            [
                ssm_x[step], gate_z[step], ssm_b[step], ssm_c[step], dt_pieces[step], ids_wide,
                jnp.zeros((SLOTS, 128 - 48), BF16),
            ],
            axis=1,
        )

    width = 2 * WIDTH + 3 * 128
    pack_one = jnp.concatenate([pack(1), own_residual[1], jnp.zeros((SLOTS, 128), BF16)], axis=1)
    to_owner = (lax.iota(jnp.int32, OWNERS)[:, None] == (back_one // SLOTS)[None, :]).astype(BF16)
    row_one = jnp.dot(to_owner, pack_one, preferred_element_type=F32).astype(BF16)
    message = jnp.concatenate(
        [
            row_one.reshape(OWNERS, SLOTS, 256),
            jnp.broadcast_to(pack(2)[None], (OWNERS, SLOTS, width)),
        ],
        axis=2,
    )
    got = lax.all_to_all(message, "req", split_axis=0, concat_axis=0, tiled=True)
    residual_two = lax.all_to_all(
        jnp.broadcast_to(own_residual[2][None], (OWNERS, SLOTS, WIDTH)),
        "req", split_axis=0, concat_axis=0, tiled=True,
    )
    home_one = select(next_one // SLOTS, got[:, :, :256].reshape(OWNERS, 2048))
    all_two = got[:, :, 256:].reshape(REQUESTS, width)
    home_two = select(next_two, all_two)
    home_residual = jnp.stack(
        [own_residual[0], home_one[:, width : width + WIDTH], select(next_two, residual_two.reshape(REQUESTS, WIDTH))]
    )

    def unpack(first, low, high):
        return jnp.stack([first, home_one[:, low:high], home_two[:, low:high]])

    x = unpack(ssm_x[0], 0, WIDTH)
    z = unpack(gate_z[0], WIDTH, 2 * WIDTH)
    b = unpack(ssm_b[0], 2 * WIDTH, 2 * WIDTH + 128)
    c = unpack(ssm_c[0], 2 * WIDTH + 128, 2 * WIDTH + 256)
    dt_parts = unpack(dt_pieces[0], 2 * WIDTH + 256, 2 * WIDTH + 280).astype(F32)
    dt = dt_parts[:, :, 0:8] + dt_parts[:, :, 8:16] + dt_parts[:, :, 16:24]

    def by_slot(value):
        return jnp.pad(jnp.transpose(value, (1, 0, 2)).astype(F32), ((0, 0), (0, 8 - STEPS), (0, 0)))

    b_slots, c_slots = by_slot(b), by_slot(c)
    state_rows = states.reshape(SLOTS, HEADS * HSIZE, NSTATE)
    parts, outer, keep = mamba(
        state_rows, x, z, b_slots, c_slots, dt, decay_rate[None], skip_gain[None], ssm_gain[None], out_weight
    )

    order_one = lax.dynamic_slice(tables, (0, me * SLOTS), (1, SLOTS))[0]
    order_two = lax.dynamic_slice(tables, (1, me // 4 * OWNERS), (1, OWNERS))[0]
    order_three = lax.dynamic_slice(tables, (2, me * SLOTS), (1, SLOTS))[0]
    pieces = update_states(order_one, state_rows, outer, keep, b_slots)
    pieces = lax.all_to_all(
        pieces.reshape(OWNERS, 2 * HSIZE, NSTATE), "req", split_axis=0, concat_axis=0, tiled=True
    )
    pieces = lax.all_to_all(
        reorder_states(order_two, pieces), "req", split_axis=0, concat_axis=0, tiled=True
    )
    final_states = place_states(order_three, pieces.reshape(SLOTS, HEADS * HSIZE, NSTATE)).reshape(states.shape)

    terms = lax.all_to_all(parts, "head", split_axis=0, concat_axis=0, tiled=True)
    projected = jnp.sum(terms.astype(F32), axis=0).reshape(STEPS, SLOTS, WIDTH)
    stream = (home_residual.astype(F32) + projected).astype(BF16).reshape(STEPS * SLOTS, WIDTH)
    streams = lax.all_to_all(
        jnp.broadcast_to(stream[None], (OWNERS, STEPS * SLOTS, WIDTH)),
        "req", split_axis=0, concat_axis=0, tiled=True,
    ).reshape(OWNERS * STEPS * SLOTS, WIDTH)

    ids_all = all_two[:, 2 * WIDTH + 280 : 2 * WIDTH + 304].astype(jnp.int32).reshape(OWNERS, SLOTS, STEPS, 8)
    wanted = me * 2 + lax.iota(jnp.int32, 2)
    named = jnp.any(ids_all[None] == wanted[:, None, None, None, None], axis=4).astype(jnp.int32)
    rank = jnp.cumsum(named, axis=2) - named
    code = jnp.where(named > 0, rank, -1)
    code = jnp.transpose(code, (0, 3, 1, 2)).reshape(2, STEPS, REQUESTS).astype(BF16)
    every_one = first_dest
    every_two = lookup(first_dest, second_dest)
    slot_of = jnp.stack([lax.iota(jnp.int32, REQUESTS), every_one, every_two])
    code_home = jnp.stack(
        [code[:, 0]]
        + [
            jnp.dot(code[:, step], one_hot(slot_of[step], REQUESTS).T, preferred_element_type=F32).astype(BF16)
            for step in (1, 2)
        ],
        axis=1,
    ).astype(jnp.int32)
    target = (slot_of[None] // SLOTS * STEPS + lax.iota(jnp.int32, STEPS)[None, :, None]) * CAP + code_home
    target = jnp.where(code_home >= 0, target, -1)
    target = jnp.transpose(target.reshape(2, STEPS, OWNERS, SLOTS), (0, 2, 1, 3)).reshape(2, OWNERS * STEPS * SLOTS)
    per_expert = OWNERS * STEPS * CAP
    pick = (lax.iota(jnp.int32, per_expert)[None, :, None] == target[:, None, :]).astype(BF16)
    pick = pick.reshape(2 * per_expert, OWNERS * STEPS * SLOTS)

    terms = expand(pick, streams, ffn_gain[None], gate_weight, up_weight)
    terms = lax.all_to_all(
        terms.reshape(HEADS, per_expert * 2 // HEADS, 2176), "head", split_axis=0, concat_axis=0, tiled=True
    )
    hidden = lax.all_gather(hidden_units(terms), "head").reshape(2, per_expert, 1024)
    served = jnp.einsum("erf,efd->erd", hidden, down_weight, preferred_element_type=F32).astype(BF16)
    served = jnp.transpose(served.reshape(2, OWNERS, STEPS * CAP, WIDTH), (1, 0, 2, 3))
    returned = lax.all_to_all(
        served.reshape(OWNERS, 2 * STEPS * CAP, WIDTH), "req", split_axis=0, concat_axis=0, tiled=True
    ).reshape(OWNERS * 2 * STEPS * CAP, WIDTH)

    same = route_ids[:, :, :, None, None] == route_ids[:, None, None, :, :]
    earlier = (lax.iota(jnp.int32, SLOTS)[None, :] < lax.iota(jnp.int32, SLOTS)[:, None])[None, :, None, :, None]
    own_rank = jnp.sum((same & earlier).astype(jnp.int32), axis=(3, 4))
    place = (route_ids * STEPS + lax.iota(jnp.int32, STEPS)[:, None, None]) * CAP + own_rank
    hit = place[:, :, :, None] == lax.iota(jnp.int32, OWNERS * 2 * STEPS * CAP)
    mixing = jnp.sum(jnp.where(hit, route_weights[:, :, :, None], 0.0), axis=2)
    mixing = mixing.reshape(STEPS * SLOTS, OWNERS * 2 * STEPS * CAP)
    sources = jnp.concatenate([own, back_one, back_two])
    steps = jnp.repeat(lax.iota(jnp.int32, STEPS), SLOTS)
    kept_rows = (sources // SLOTS * STEPS + steps) * SLOTS + sources % SLOTS
    stream_own = jnp.dot(one_hot(kept_rows, OWNERS * STEPS * SLOTS), streams, preferred_element_type=F32)
    mixed = stream_own + jnp.dot(
        mixing, returned.astype(F32), precision=lax.Precision.HIGHEST, preferred_element_type=F32
    )
    return mixed.astype(BF16).reshape(STEPS, SLOTS, WIDTH), final_states


def solution(mesh):
    placed = (
        P("req", "head", None, None),
        P(None, "req", "head"),
        P(None, "req", "head"),
        P(None, "req", "head"),
        P(None, "req", "head"),
        P(None, "req", "head"),
        P("head"),
        P("head"),
        P("head"),
        P("head", None),
        P(None, "req", None),
        P("head"),
        P(None, "req", None),
        P(None, "req", None),
        P("req", "head", None),
        P("req", "head", None),
        P("req", None, "head"),
        P(),
    )
    return jax.shard_map(
        shards,
        mesh=mesh,
        in_specs=placed,
        out_specs=(P(None, "req", "head"), P("req", "head", None, None)),
        check_vma=False,
    )
```

```python
import functools

import jax
import jax.numpy as jnp
from jax import lax
from jax.experimental import pallas as pl
from jax.experimental.pallas import tpu as pltpu
from jax.sharding import PartitionSpec as P

NSTATE = 128
EXPERTS = 64
STEPS = 3
CAP = 2
OWNERS = 32
SLOTS = 8
REQUESTS = OWNERS * SLOTS
HEADS = 8
HSIZE = 64
WIDTH = 512
FFE = 1024
ROWS = STEPS * SLOTS
TERMS = 2 * FFE + 128
CHUNK = 48
NORM_EPS = 1e-05
F32 = jnp.float32
BF16 = jnp.bfloat16
VMEM_SPEC = pl.BlockSpec(memory_space=pltpu.VMEM)
HBM_SPEC = pl.BlockSpec(memory_space=pltpu.HBM)


def params(mebibytes):
    return pltpu.CompilerParams(vmem_limit_bytes=mebibytes * 2**20)


def cost(flops, moved):
    return pl.CostEstimate(flops=flops, bytes_accessed=moved, transcendentals=0)


def run_kernel(body, args, outs, name, scratch=(), flops=0, moved=2**20, out_specs=None, limit=24):
    count, made = len(args), len(outs)
    modes = [mode for _, mode in args]
    copied = [i for i, mode in enumerate(modes) if mode in "hls"]

    def kernel(*refs):
        ins = list(refs[:count])
        results = refs[count : count + made]
        rest = refs[count + made :]
        copies = {}
        for position, i in enumerate(copied):
            copies[i] = pltpu.make_async_copy(ins[i], rest[position], rest[len(copied)].at[position])
            ins[i] = rest[position]
        for copy in copies.values():
            copy.start()
        for i, copy in copies.items():
            if modes[i] != "l":
                copy.wait()
        own = rest[len(copied) + 1 :] if copied else rest
        body(ins, results, own, lambda i: copies[i].wait())

    spaces = [(pltpu.SMEM if modes[i] == "s" else pltpu.VMEM)(args[i][0].shape, args[i][0].dtype) for i in copied]
    if copied:
        spaces.append(pltpu.SemaphoreType.DMA((len(copied),)))
    return pl.pallas_call(
        kernel,
        out_shape=tuple(outs),
        in_specs=[VMEM_SPEC if mode == "v" else HBM_SPEC for mode in modes],
        out_specs=tuple(out_specs or [VMEM_SPEC] * made),
        scratch_shapes=spaces + list(scratch),
        compiler_params=params(limit),
        cost_estimate=cost(flops, moved),
        name=name,
    )(*[array for array, _ in args])


def shaped(shape, dtype):
    return jax.ShapeDtypeStruct(shape, dtype)


def split_pair(value):
    high = value.astype(BF16)
    low = (value - high.astype(F32)).astype(BF16)
    return high, low


def contract(a, b, dims=((1,), (0,))):
    return lax.dot_general(a, b, (dims, ((), ())), preferred_element_type=F32)


def iota(shape, dim):
    return lax.broadcasted_iota(jnp.int32, shape, dim)


def hot(condition):
    return jnp.where(condition, 1.0, 0.0).astype(BF16)


def silu(value):
    return value / (1.0 + jnp.exp(-value))


def plan_kernel(ins, outs, scratch, wait):
    (dest_ref,), (table_ref,) = ins, outs
    size = (REQUESTS, REQUESTS)
    row_id = iota(size, 1)
    col_id = iota(size, 0)
    first_row = jnp.broadcast_to(dest_ref[0:1, :], size)
    second_row = jnp.broadcast_to(dest_ref[1:2, :], size)
    first_col = jnp.transpose(first_row)
    second_col = jnp.transpose(second_row).astype(F32).astype(BF16)
    final_col = contract(hot(first_col == row_id), second_col).astype(jnp.int32)
    final_row = jnp.transpose(final_col)
    differs = row_id != col_id
    color_col = jnp.zeros(size, jnp.int32)
    color_row = color_col
    for level in (1, 2, 3):
        alike = (color_col == color_row) & differs
        source = hot(((row_id >> level) == (col_id >> level)) & alike)
        target = hot(((final_row >> level) == (final_col >> level)) & alike)
        power = contract(source, target).astype(BF16)
        least = col_id.astype(F32)
        for turn in range(7):
            least = jnp.minimum(least, contract(power, least.astype(BF16)))
            if turn < 6:
                power = contract(power, power).astype(BF16)
        other = contract(source, least.astype(BF16))
        color_col = color_col * 2 + jnp.where(least > other, 1, 0)
        color_row = jnp.transpose(color_col)

    def lookup(key, value):
        return jnp.sum(jnp.where(key == row_id, value, 0), axis=0, keepdims=True)

    table_ref[...] = jnp.zeros_like(table_ref)
    table_ref[0:1, :] = lookup((col_id & -8) + color_col, col_id & 7)
    table_ref[1:2, :] = lookup(color_col * OWNERS + (final_col >> 3), col_id >> 3)
    table_ref[2:3, :] = lookup(final_col, color_col)


def routing_tables(dest):
    outs = [shaped((8, REQUESTS), jnp.int32)]
    return run_kernel(plan_kernel, [(dest, "h")], outs, "plan_states", flops=2 * 10**9)[0]


LAST = 24
PIECES = 15
MESSAGE = LAST + PIECES * SLOTS


def place_pieces(value):
    parts = []
    rest = value
    for _ in range(2):
        high = rest.astype(BF16)
        parts.append(high)
        rest = rest - high.astype(F32)
    parts.append(rest.astype(BF16))
    total = jnp.zeros((SLOTS, 128), F32)
    for piece in range(3):
        spot = hot(iota((8, 128), 1) == iota((8, 128), 0) + 8 * piece)
        total = total + contract(parts[piece], spot)
    return total


def join_pieces(block):
    spot = hot((iota((128, 8), 0) % 8 == iota((128, 8), 1)) & (iota((128, 8), 0) < 24))
    return contract(block.astype(BF16), spot)


def read_rows(pack_ref, first):
    return jnp.concatenate([pack_ref[:, first + piece, :] for piece in range(4)], axis=1)


def sender_match(dest_row, me):
    slot = iota((SLOTS, REQUESTS), 0) + me * SLOTS
    owner = hot((iota((REQUESTS, OWNERS), 0) >> 3) == iota((REQUESTS, OWNERS), 1))
    return contract(hot(jnp.broadcast_to(dest_row, slot.shape) == slot), owner).astype(BF16)


def pack_kernel(ins, outs, scratch, wait):
    dest_ref, x_ref, z_ref, residual_ref, b_ref, c_ref, dt_ref, ids_ref = ins
    (message_ref,), (wide_ref, last_ref) = outs, scratch
    me = lax.axis_index("req")
    columns = pl.ds(pl.multiple_of(lax.axis_index("head") * WIDTH, WIDTH), WIDTH)
    back = sender_match(dest_ref[0:1, :], me)

    def pieces(step):
        wide = [x_ref[step], z_ref[step], residual_ref[step, :, columns]]
        cut = [value[:, 128 * i : 128 * (i + 1)] for value in wide for i in range(4)]
        return cut + [b_ref[step], c_ref[step], place_pieces(dt_ref[step]).astype(BF16)]

    one = pieces(1)
    two = pieces(2)
    wide_ref[:, PIECES:LAST, :] = jnp.zeros((OWNERS, LAST - PIECES, 128), F32)
    for row in range(PIECES):
        wide_ref[:, row, :] = contract(back, one[row], ((0,), (0,)))
    ids = jnp.zeros((SLOTS, 128), F32)
    for step in range(STEPS):
        spot = hot(iota((8, 128), 1) == iota((8, 128), 0) + 8 * (step + 3))
        ids = ids + contract(ids_ref[step].astype(F32).astype(BF16), spot)
    wide_ref[:, LAST:32, :] = jnp.broadcast_to(two[0].astype(F32)[None], (OWNERS, SLOTS, 128))
    for row in range(1, PIECES):
        value = two[row].astype(F32)
        if row == PIECES - 1:
            value = value + ids
        last_ref[(row - 1) * SLOTS : row * SLOTS, :] = value
    message_ref[:, 0:32, :] = wide_ref[...].astype(BF16)
    last = last_ref[...].astype(BF16)
    message_ref[:, 32:MESSAGE, :] = jnp.broadcast_to(last[None], (OWNERS,) + last.shape)


def pack_inputs(*arrays):
    outs = [shaped((OWNERS, MESSAGE, 128), BF16)]
    scratch = [pltpu.VMEM((OWNERS, 32, 128), F32), pltpu.VMEM((MESSAGE - 32, 128), F32)]
    return run_kernel(pack_kernel, [(array, "h") for array in arrays], outs, "pack_inputs", scratch, limit=58)[0]


def head_spread():
    return hot(iota((HEADS, WIDTH), 1) // HSIZE == iota((HEADS, WIDTH), 0))


def widen(value, spread):
    parts = []
    rest = value
    for _ in range(3):
        high = rest.astype(BF16)
        parts.append(high)
        rest = rest - high.astype(F32)
    return contract(parts[0], spread) + contract(parts[1], spread) + contract(parts[2], spread)


def softplus(value):
    return jnp.maximum(value, 0.0) + jnp.log1p(jnp.exp(-jnp.abs(value)))


def mamba_kernel(ins, outs, scratch, wait):
    dest_ref, got_ref, state_ref, x_ref, z_ref, residual_ref, b_ref, c_ref, dt_ref = ins[:9]
    decay_ref, skip_ref, gain_ref, weight_ref = ins[9:]
    keep_ref, send_ref, residual_out_ref, outer_ref, kept_ref, b_rows_ref = outs
    wide_ref, rows_in_ref, c_rows_ref, read_ref, rows_ref = scratch
    me = lax.axis_index("req")
    column = lax.axis_index("head")
    for slot in range(SLOTS):
        middle = dest_ref[0, me * SLOTS + slot]
        final = dest_ref[1, middle]
        rows_in_ref[slot, 0:16, :] = got_ref[middle // SLOTS, 0:16, :].astype(F32)
        wide_ref[slot] = got_ref[final // SLOTS].astype(F32)
        rows_in_ref[slot, 16 : 16 + PIECES, :] = wide_ref[
            slot, pl.ds(LAST + final % SLOTS, PIECES, stride=SLOTS), :
        ]
    xs = [x_ref[0].astype(F32), read_rows(rows_in_ref, 0), read_rows(rows_in_ref, 16)]
    zs = [z_ref[0].astype(F32), read_rows(rows_in_ref, 4), read_rows(rows_in_ref, 20)]
    steps_b = [b_ref[0].astype(F32), rows_in_ref[:, 12, :], rows_in_ref[:, 28, :]]
    steps_c = [c_ref[0].astype(F32), rows_in_ref[:, 13, :], rows_in_ref[:, 29, :]]
    raws = [dt_ref[0], join_pieces(rows_in_ref[:, 14, :]), join_pieces(rows_in_ref[:, 30, :])]
    own_columns = pl.ds(pl.multiple_of(column * WIDTH, WIDTH), WIDTH)
    residual_out_ref[0:8, :] = residual_ref[0, :, own_columns].astype(F32)
    residual_out_ref[8:16, :] = read_rows(rows_in_ref, 8)
    residual_out_ref[16:24, :] = read_rows(rows_in_ref, 24)

    c_rows_ref[...] = jnp.zeros_like(c_rows_ref)
    for step in range(STEPS):
        c_rows_ref[:, step, :] = steps_c[step]
    across = ((1,), (1,))
    wait(2)
    for slot in range(SLOTS):
        high, low = split_pair(state_ref[slot])
        c_rows = c_rows_ref[slot].astype(BF16)
        read_ref[slot] = contract(c_rows, high, across) + contract(c_rows, low, across)
    spread = head_spread()
    skip = widen(jnp.broadcast_to(skip_ref[...], (SLOTS, HEADS)), spread)
    inputs, kept = [], []
    for step in range(STEPS):
        step_size = softplus(raws[step])
        kept.append(widen(jnp.exp(-decay_ref[...] * step_size), spread))
        inputs.append(widen(step_size, spread) * xs[step])
    for step in range(STEPS):
        total = read_ref[:, step, :] * kept[0]
        for earlier in range(step + 1):
            if earlier > 0:
                total = total * kept[earlier]
            match = jnp.sum(steps_b[earlier] * steps_c[step], axis=1, keepdims=True)
            total = total + inputs[earlier] * match
        gated = (total + skip * xs[step]) * silu(zs[step])
        scale = lax.rsqrt(jnp.mean(gated * gated, axis=1, keepdims=True) + NORM_EPS)
        rows_ref[step * SLOTS : (step + 1) * SLOTS, :] = gated * scale * gain_ref[...]
    rows = rows_ref[...].astype(BF16)
    wait(12)
    for turn in range(HEADS):
        block = 2 * ((column // 2 + turn) % 4) + (column + turn // 4) % 2
        columns = pl.ds(pl.multiple_of(block * WIDTH, WIDTH), WIDTH)
        terms = contract(rows, weight_ref[:, columns]).astype(BF16)
        if turn < 4:
            keep_ref[turn] = terms
        else:
            send_ref[turn - 4] = terms
    late = kept[2]
    factors = [inputs[0] * (kept[1] * late), inputs[1] * late, inputs[2]]
    outer_ref[...] = jnp.zeros_like(outer_ref)
    kept_ref[...] = jnp.zeros_like(kept_ref)
    b_rows_ref[...] = jnp.zeros_like(b_rows_ref)
    for step in range(STEPS):
        outer_ref[:, step, :] = factors[step]
        b_rows_ref[:, step, :] = steps_b[step]
    kept_ref[:, 0, :] = kept[0] * (kept[1] * late)


def mamba(dest, got, state, *arrays):
    part = shaped((4, ROWS, WIDTH), BF16)
    factor = shaped((SLOTS, 8, WIDTH), F32)
    outs = [part, part, shaped((ROWS, WIDTH), F32), factor, factor, shaped((SLOTS, 8, NSTATE), F32)]
    scratch = [
        pltpu.VMEM((SLOTS, MESSAGE, 128), F32),
        pltpu.VMEM((SLOTS, 32, 128), F32),
        pltpu.VMEM((SLOTS, 8, NSTATE), F32),
        pltpu.VMEM((SLOTS, 8, WIDTH), F32),
        pltpu.VMEM((ROWS, WIDTH), F32),
    ]
    args = [(dest, "s"), (got, "v"), (state, "l")] + [(array, "h") for array in arrays[:-1]] + [(arrays[-1], "l")]
    return run_kernel(mamba_kernel, args, outs, "mamba_steps", scratch, 2 * 24 * 512 * 4096, 8 * 2**20, limit=54)


def update_kernel(ins, outs, scratch, wait):
    table_ref, state_any, outer_ref, keep_ref, b_ref = ins
    (out_any,), (state_ref, made_ref, in_sems, out_sems) = outs, scratch
    first = lax.axis_index("req") * SLOTS
    sources = [table_ref[0, first + block] for block in range(SLOTS)]
    loads = [
        pltpu.make_async_copy(state_any.at[sources[block]], state_ref.at[block], in_sems.at[block])
        for block in range(SLOTS)
    ]
    for load in loads:
        load.start()
    stores = []
    ones = jnp.ones((8, NSTATE), BF16)
    along = ((0,), (0,))
    for block in range(SLOTS):
        b_rows = b_ref[sources[block]].astype(BF16)
        outer_high, outer_low = split_pair(outer_ref[sources[block]])
        keep_high, keep_low = split_pair(keep_ref[sources[block]])
        keep = contract(keep_high, ones, along) + contract(keep_low, ones, along)
        added = contract(outer_high, b_rows, along) + contract(outer_low, b_rows, along)
        loads[block].wait()
        made_ref[block] = (keep * state_ref[block] + added).astype(BF16)
        store = pltpu.make_async_copy(made_ref.at[block], out_any.at[block], out_sems.at[block])
        store.start()
        stores.append(store)
    for store in stores:
        store.wait()


def update_states(table, state, factors):
    scratch = [
        pltpu.VMEM(state.shape, F32),
        pltpu.VMEM(state.shape, BF16),
        pltpu.SemaphoreType.DMA((SLOTS,)),
        pltpu.SemaphoreType.DMA((SLOTS,)),
    ]
    args = [(table, "s"), (state, "m")] + [(factor, "h") for factor in factors]
    return run_kernel(
        update_kernel, args, [shaped(state.shape, BF16)], "update_states", scratch,
        2 * 32 * 512 * 1024, 3 * 2**20, [HBM_SPEC],
    )[0]


CORES = [(i, i ^ 1) for i in range(HEADS)]


def along_y(value, distance):
    moves = [(i, ((i // 2 + distance) % 4) * 2 + i % 2) for i in range(HEADS)]
    return lax.ppermute(value, "head", moves)


def add_kernel(tail, ins, outs, scratch, wait):
    keep_ref, got_ref = ins
    first_ref, *rest_refs = outs
    for turn in range(4):
        total = keep_ref[turn].astype(F32) + got_ref[turn].astype(F32)
        if turn == 0:
            first_ref[...] = total
            continue
        out_ref = rest_refs[turn - 1]
        if tail:
            out_ref[:, : 2 * FFE] = total[:, : 2 * FFE].astype(BF16)
            out_ref[:, 2 * FFE :] = pair_lanes(jnp.sum(total[:, 2 * FFE :], axis=1, keepdims=True))
        else:
            out_ref[...] = total.astype(BF16)


def pair_lanes(value):
    high, low = split_pair(value)
    shape = (value.shape[0], 128)
    lane = iota(shape, 1)
    high_wide = jnp.broadcast_to(high.astype(F32), shape)
    low_wide = jnp.broadcast_to(low.astype(F32), shape)
    return jnp.where(lane == 0, high_wide, jnp.where(lane == 1, low_wide, 0.0)).astype(BF16)


def add_cores(keep, got, tail):
    shape = keep.shape[1:]
    outs = [shaped(shape, F32)] + [shaped(shape, BF16)] * 3
    return run_kernel(
        functools.partial(add_kernel, tail), [(keep, "v"), (got, "v")], outs, "add_cores", moved=4 * keep.size
    )


def scatter_sum(keep, send, tail, beside=None):
    got = lax.ppermute(send, "head", CORES)
    first, *rest = add_cores(keep, got, tail)
    if beside is not None:
        first, beside, *rest = lax.optimization_barrier((first, beside, *rest))
        beside = exchange(beside)
    far = along_y(rest[1], 2)
    near = along_y(rest[0], 1)
    other = along_y(rest[2], 3)
    return (first, near, far, other), beside


def stream_kernel(ins, outs, scratch, wait):
    first_ref, a_ref, b_ref, c_ref, residual_ref = ins
    (out_ref,) = outs
    total = first_ref[...] + a_ref[...].astype(F32) + b_ref[...].astype(F32) + c_ref[...].astype(F32)
    stream = (residual_ref[...] + total).astype(BF16)
    out_ref[...] = jnp.broadcast_to(stream[None], out_ref.shape)


def stream_copies(parts, residual):
    args = [(part, "v") for part in parts] + [(residual, "v")]
    return run_kernel(stream_kernel, args, [shaped((OWNERS, ROWS, WIDTH), BF16)], "stream_copies")[0]


def routes_kernel(ins, outs, scratch, wait):
    dest_ref, got_ref, ids_ref, weights_ref = ins
    pick_ref, kept_ref, high_ref, low_ref = outs
    me = lax.axis_index("req")
    column = lax.axis_index("head")
    total_rows = OWNERS * ROWS
    square = (REQUESTS, REQUESTS)
    row_id = iota(square, 1)
    col_id = iota(square, 0)
    first = dest_ref[0:1, :]
    second = jnp.broadcast_to(dest_ref[1:2, :], (8, REQUESTS)).astype(F32).astype(BF16)
    hop_one = hot(jnp.broadcast_to(first, square) == col_id)
    both = contract(second, hop_one)[0:1, :].astype(jnp.int32)
    hops = [hot(row_id == col_id), hop_one, hot(jnp.broadcast_to(both, square) == col_id)]
    slots = [iota((1, REQUESTS), 1), first, both]
    spread = []
    for step in range(STEPS):
        shape = (REQUESTS, total_rows)
        g = iota(shape, 0)
        spread.append(hot(iota(shape, 1) == (g >> 3) * ROWS + step * SLOTS + (g & 7)))
    at_row = jnp.zeros((8, total_rows), F32)
    for step in range(STEPS):
        wide = jnp.broadcast_to(slots[step], (8, REQUESTS)).astype(F32).astype(BF16)
        at_row = at_row + contract(wide, spread[step])
    ids = got_ref[:, MESSAGE - 16 :, :].astype(F32)[:, SLOTS:, :].reshape(REQUESTS, 128)
    step_of = hot((iota((128, 128), 0) >> 3) == iota((128, 128), 1) + 3)
    earlier = hot(((row_id >> 3) == (col_id >> 3)) & (row_id < col_id))
    slot = iota((REQUESTS, 128), 0)
    lane = iota((REQUESTS, 128), 1)
    owner = slot >> 3
    part = owner >> 2
    turn = (((part & 1) + column) & 1) * 4 + (((part >> 1) - (column >> 1)) & 3)
    base = turn * (CHUNK // 2) + (owner & 3) * (STEPS * CAP) + lane * CAP
    for expert in range(2):
        match = (ids == (me * 2 + expert).astype(F32)) & (lane >= 24) & (lane < 48)
        named = contract(hot(match), step_of)
        rank = contract(earlier, named.astype(BF16))
        target = jnp.where(named > 0.5, base.astype(F32) + rank + 1.0, 0.0).astype(BF16)
        row = jnp.zeros((8, total_rows), F32)
        for step in range(STEPS):
            select = hot(iota((8, 128), 1) == step)
            by_slot = contract(select, target, ((1,), (1,)))
            by_home = contract(by_slot.astype(BF16), hops[step])
            row = row + contract(by_home.astype(BF16), spread[step])
        half = OWNERS * STEPS * CAP
        want = iota((half, total_rows), 0).astype(F32) + 1.0
        pick_ref[expert * half : (expert + 1) * half, :] = hot(jnp.broadcast_to(row[0:1, :], (half, total_rows)) == want)
    shape = (ROWS, total_rows)
    mine = (me * SLOTS + iota(shape, 0) % SLOTS).astype(F32)
    step_match = (iota(shape, 1) % ROWS) // SLOTS == iota(shape, 0) // SLOTS
    kept_ref[...] = hot((jnp.broadcast_to(at_row[0:1, :], shape) == mine) & step_match)
    expert_lane = iota((ROWS, 128), 1)
    chosen = jnp.zeros((ROWS, 128), F32)
    weight = jnp.zeros((ROWS, 128), F32)
    for choice in range(8):
        hit = expert_lane == ids_ref[:, choice : choice + 1]
        chosen = chosen + jnp.where(hit, 1.0, 0.0)
        weight = weight + jnp.where(hit, weights_ref[:, choice : choice + 1], 0.0)
    small = (ROWS, ROWS)
    before = hot((iota(small, 0) // SLOTS == iota(small, 1) // SLOTS) & (iota(small, 1) < iota(small, 0)))
    rank = contract(before, chosen.astype(BF16))
    span = OWNERS * CHUNK
    place = iota((128, span), 1) % CHUNK % 12
    expert_of = 2 * (iota((128, span), 1) // CHUNK) + place // 6
    to_place = hot(iota((128, span), 0) == expert_of)
    spot = iota((ROWS, span), 1) % CHUNK
    fits = (contract(rank.astype(BF16), to_place) == (spot % 2).astype(F32)) & (
        (spot % 6) // 2 == iota((ROWS, span), 0) // SLOTS
    )
    for value, out_ref in zip(split_pair(weight), (high_ref, low_ref)):
        value = jnp.where(fits, contract(value, to_place), 0.0)
        for piece in range(4):
            out_ref[piece] = jnp.where(spot // 12 == piece, value, 0.0).astype(BF16)


def routes(dest, got, ids, weights):
    total_rows = OWNERS * ROWS
    mixing = shaped((4, ROWS, OWNERS * CHUNK), BF16)
    outs = [
        shaped((2 * OWNERS * STEPS * CAP, total_rows), BF16),
        shaped((ROWS, total_rows), BF16),
        mixing,
        mixing,
    ]
    args = [(dest, "h"), (got, "v"), (ids, "h"), (weights, "h")]
    return run_kernel(routes_kernel, args, outs, "routes", flops=10**9)


def expand_kernel(ins, outs, scratch, wait):
    pick_ref, stream_ref, gain_ref, gate_ref, up_ref = ins
    keep_ref, send_ref = outs
    half = pick_ref.shape[0] // 2
    some = CHUNK // 2
    for expert in range(2):
        picked = contract(pick_ref[expert * half : (expert + 1) * half, :], stream_ref[...])
        tail = pair_lanes(jnp.sum(picked * picked, axis=1, keepdims=True))
        scaled = (picked * gain_ref[...]).astype(BF16)
        if expert == 0:
            wait(3)
            wait(4)
        values = [
            contract(scaled, gate_ref[expert]).astype(BF16),
            contract(scaled, up_ref[expert]).astype(BF16),
            tail,
        ]
        rows = slice(expert * some, (expert + 1) * some)
        for turn in range(HEADS):
            out_ref = keep_ref if turn < 4 else send_ref
            source = slice(turn * some, (turn + 1) * some)
            for value, start in zip(values, (0, FFE, 2 * FFE)):
                out_ref[turn % 4, rows, start : start + value.shape[1]] = value[source, :]


def expand(pick, stream, gain, gate_weight, up_weight):
    part = shaped((4, CHUNK, TERMS), BF16)
    args = [(pick, "h"), (stream, "v"), (gain, "h"), (gate_weight, "l"), (up_weight, "l")]
    return run_kernel(
        expand_kernel, args, [part, part], "expand_experts", flops=2 * 384 * 512 * (2048 + 768), moved=8 * 2**20
    )


def hidden_kernel(ins, outs, scratch, wait):
    first_ref, a_ref, b_ref, c_ref = ins
    (out_ref,) = outs
    total = first_ref[...] + a_ref[...].astype(F32) + b_ref[...].astype(F32) + c_ref[...].astype(F32)
    square = jnp.sum(total[:, 2 * FFE :], axis=1, keepdims=True)
    inverse = lax.rsqrt(square * (1.0 / (HEADS * WIDTH)) + NORM_EPS)
    out_ref[...] = (silu(total[:, :FFE] * inverse) * (total[:, FFE : 2 * FFE] * inverse)).astype(BF16)


def hidden_units(parts):
    args = [(part, "v") for part in parts]
    return run_kernel(hidden_kernel, args, [shaped((CHUNK, FFE), BF16)], "hidden_units")[0]


def shrink_kernel(ins, outs, scratch, wait):
    table_ref, pieces_ref, weight_ref, *hidden_refs = ins
    (out_ref,), (sems,) = outs, scratch
    first = lax.axis_index("req") // 4 * OWNERS
    column = lax.axis_index("head")
    moves = [
        pltpu.make_async_copy(
            pieces_ref.at[table_ref[1, first + block]],
            out_ref.at[block, pl.ds(CHUNK, 2 * HSIZE), :],
            sems.at[block],
        )
        for block in range(OWNERS)
    ]
    for move in moves:
        move.start()
    hidden = jnp.concatenate([ref[...] for ref in hidden_refs], axis=0)
    wait(2)
    served = [contract(hidden, weight_ref[expert]) for expert in range(2)]
    shape = (4 * 16, CHUNK)
    row, source = iota(shape, 0), iota(shape, 1)
    inside = row % 16
    spot = hot((inside < 12) & (source == (inside // 6) * (CHUNK // 2) + (row // 16) * 6 + inside % 6))
    half = iota((CHUNK, WIDTH), 0) < CHUNK // 2
    for turn in range(HEADS):
        rows = slice(turn * CHUNK, (turn + 1) * CHUNK)
        chunk = jnp.where(half, served[0][rows], served[1][rows]).astype(BF16)
        owner = (2 * ((column // 2 - turn + 8) % 4) + (column + turn // 4) % 2) * 4
        block = contract(spot, chunk)
        for piece in range(4):
            wide = block[piece * 16 : piece * 16 + 12, :]
            cut = [wide[:, 128 * i : 128 * (i + 1)] for i in range(4)]
            out_ref[owner + piece, 0:CHUNK, :] = jnp.concatenate(cut, axis=0).astype(BF16)
    for move in moves:
        move.wait()


def shrink(table, pieces, hidden, weight):
    args = [(table, "s"), (pieces, "m"), (weight, "l")] + [(block, "v") for block in hidden]
    outs = [shaped((OWNERS, CHUNK + 2 * HSIZE, 128), BF16)]
    return run_kernel(
        shrink_kernel, args, outs, "shrink_experts", [pltpu.SemaphoreType.DMA((OWNERS,))],
        2 * 2 * 384 * 1024 * 512, 4 * 2**20,
    )[0]


def finish_kernel(ins, outs, scratch, wait):
    table_ref, back_ref, high_ref, low_ref, kept_ref, stream_ref = ins
    mixed_ref, states_any = outs
    made_ref, sems = scratch
    first = lax.axis_index("req") * SLOTS
    stores = []
    for slot in range(SLOTS):
        color = table_ref[2, first + slot]
        for piece in range(4):
            rows = slice(piece * 2 * HSIZE, (piece + 1) * 2 * HSIZE)
            made_ref[slot, rows, :] = back_ref[color * 4 + piece, CHUNK:, :].astype(F32)
        store = pltpu.make_async_copy(made_ref.at[slot], states_any.at[slot], sems.at[slot])
        store.start()
        stores.append(store)
    served = back_ref[:, 0:CHUNK, :].reshape(OWNERS * CHUNK, 128)
    for ref in (2, 3, 4, 5):
        wait(ref)
    stream = contract(kept_ref[...], stream_ref[...])
    for piece in range(4):
        columns = slice(piece * 128, (piece + 1) * 128)
        mixed = contract(high_ref[piece], served) + contract(low_ref[piece], served)
        mixed_ref[:, columns] = (stream[:, columns] + mixed).astype(BF16)
    for store in stores:
        store.wait()


def finish(table, back, high, low, kept, streams):
    args = [(table, "s"), (back, "v"), (high, "l"), (low, "l"), (kept, "l"), (streams, "l")]
    outs = [shaped((ROWS, WIDTH), BF16), shaped((SLOTS, HEADS * HSIZE, NSTATE), F32)]
    scratch = [pltpu.VMEM((SLOTS, HEADS * HSIZE, NSTATE), F32), pltpu.SemaphoreType.DMA((SLOTS,))]
    return run_kernel(
        finish_kernel, args, outs, "finish", scratch, 10**8, 4 * 2**20, [VMEM_SPEC, HBM_SPEC]
    )


def exchange(value):
    return lax.all_to_all(value, "req", split_axis=0, concat_axis=0, tiled=True)


def shards(
    states, ssm_x, gate_z, ssm_b, ssm_c, dt_raw, decay_rate, skip_gain, ssm_gain, out_weight,
    residual, ffn_gain, route_ids, route_weights, gate_weight, up_weight, down_weight, dest,
):
    fence = lax.optimization_barrier
    state_rows = states.reshape(SLOTS, HEADS * HSIZE, NSTATE)
    own = (ssm_x, gate_z, residual, ssm_b, ssm_c, dt_raw)

    message = pack_inputs(dest, *own, route_ids)
    message, later_dest = fence((message, dest))
    got = exchange(message)
    table = routing_tables(later_dest)
    got, table = fence((got, table))

    keep_part, send_part, home_residual, *factors = mamba(
        dest, got, state_rows, *own, decay_rate[None], skip_gain[None], ssm_gain[None], out_weight
    )
    parts, _ = scatter_sum(keep_part, send_part, False)
    copies, got, factors = fence((stream_copies(parts, home_residual), got, factors))
    streams = exchange(copies).reshape(OWNERS * ROWS, WIDTH)
    routed = routes(dest, got, route_ids.reshape(ROWS, 8), route_weights.reshape(ROWS, 8))
    pieces = update_states(table, state_rows, factors)
    streams, pieces, (pick, kept, high, low) = fence((streams, pieces, routed))

    keep_part, send_part = expand(pick, streams, ffn_gain[None], gate_weight, up_weight)
    parts, pieces = scatter_sum(keep_part, send_part, True, pieces.reshape(OWNERS, 2 * HSIZE, NSTATE))
    hidden = hidden_units(parts)
    far = along_y(hidden, 2)
    near = along_y(hidden, 1)
    other = along_y(hidden, 3)
    blocks = [hidden, near, far, other]
    blocks = blocks + [lax.ppermute(block, "head", CORES) for block in blocks]
    back = exchange(shrink(table, pieces, blocks, down_weight))
    mixed, final_states = finish(table, back, high, low, kept, streams)
    return mixed.reshape(STEPS, SLOTS, WIDTH), final_states.reshape(states.shape)


def solution(mesh):
    placed = (
        P("req", "head", None, None),
        P(None, "req", "head"),
        P(None, "req", "head"),
        P(None, "req", "head"),
        P(None, "req", "head"),
        P(None, "req", "head"),
        P("head"),
        P("head"),
        P("head"),
        P("head", None),
        P(None, "req", None),
        P("head"),
        P(None, "req", None),
        P(None, "req", None),
        P("req", "head", None),
        P("req", "head", None),
        P("req", None, "head"),
        P(),
    )
    return jax.shard_map(
        shards,
        mesh=mesh,
        in_specs=placed,
        out_specs=(P(None, "req", "head"), P("req", "head", None, None)),
        check_vma=False,
    )
```

```python
import functools

import jax
import jax.numpy as jnp
from jax import lax
from jax.experimental import pallas as pl
from jax.experimental.pallas import tpu as pltpu
from jax.sharding import PartitionSpec as P

NSTATE = 128
EXPERTS = 64
STEPS = 3
CAP = 2
OWNERS = 32
SLOTS = 8
REQUESTS = OWNERS * SLOTS
HEADS = 8
HSIZE = 64
WIDTH = 512
FFE = 1024
ROWS = STEPS * SLOTS
TERMS = 2 * FFE + 128
CHUNK = 48
NORM_EPS = 1e-05
F32 = jnp.float32
BF16 = jnp.bfloat16
VMEM_SPEC = pl.BlockSpec(memory_space=pltpu.VMEM)
HBM_SPEC = pl.BlockSpec(memory_space=pltpu.HBM)


def params(mebibytes):
    return pltpu.CompilerParams(vmem_limit_bytes=mebibytes * 2**20)


def cost(flops, moved):
    return pl.CostEstimate(flops=flops, bytes_accessed=moved, transcendentals=0)


def run_kernel(body, args, outs, name, scratch=(), flops=0, moved=2**20, out_specs=None, limit=24):
    count, made = len(args), len(outs)
    modes = [mode for _, mode in args]
    copied = [i for i, mode in enumerate(modes) if mode in "hls"]

    def kernel(*refs):
        ins = list(refs[:count])
        results = refs[count : count + made]
        rest = refs[count + made :]
        copies = {}
        for position, i in enumerate(copied):
            copies[i] = pltpu.make_async_copy(ins[i], rest[position], rest[len(copied)].at[position])
            ins[i] = rest[position]
        for copy in copies.values():
            copy.start()
        for i, copy in copies.items():
            if modes[i] != "l":
                copy.wait()
        own = rest[len(copied) + 1 :] if copied else rest
        body(ins, results, own, lambda i: copies[i].wait())

    spaces = [(pltpu.SMEM if modes[i] == "s" else pltpu.VMEM)(args[i][0].shape, args[i][0].dtype) for i in copied]
    if copied:
        spaces.append(pltpu.SemaphoreType.DMA((len(copied),)))
    return pl.pallas_call(
        kernel,
        out_shape=tuple(outs),
        in_specs=[VMEM_SPEC if mode == "v" else HBM_SPEC for mode in modes],
        out_specs=tuple(out_specs or [VMEM_SPEC] * made),
        scratch_shapes=spaces + list(scratch),
        compiler_params=params(limit),
        cost_estimate=cost(flops, moved),
        name=name,
    )(*[array for array, _ in args])


def shaped(shape, dtype):
    return jax.ShapeDtypeStruct(shape, dtype)


def split_pair(value):
    high = value.astype(BF16)
    low = (value - high.astype(F32)).astype(BF16)
    return high, low


def contract(a, b, dims=((1,), (0,))):
    return lax.dot_general(a, b, (dims, ((), ())), preferred_element_type=F32)


def iota(shape, dim):
    return lax.broadcasted_iota(jnp.int32, shape, dim)


def hot(condition):
    return jnp.where(condition, 1.0, 0.0).astype(BF16)


def silu(value):
    return value / (1.0 + jnp.exp(-value))


def plan_kernel(ins, outs, scratch, wait):
    (dest_ref,), (table_ref,) = ins, outs
    size = (REQUESTS, REQUESTS)
    row_id = iota(size, 1)
    col_id = iota(size, 0)
    first_row = jnp.broadcast_to(dest_ref[0:1, :], size)
    second_row = jnp.broadcast_to(dest_ref[1:2, :], size)
    first_col = jnp.transpose(first_row)
    second_col = jnp.transpose(second_row).astype(F32).astype(BF16)
    final_col = contract(hot(first_col == row_id), second_col).astype(jnp.int32)
    final_row = jnp.transpose(final_col)
    differs = row_id != col_id
    color_col = jnp.zeros(size, jnp.int32)
    color_row = color_col
    for level in (1, 2, 3):
        alike = (color_col == color_row) & differs
        source = hot(((row_id >> level) == (col_id >> level)) & alike)
        target = hot(((final_row >> level) == (final_col >> level)) & alike)
        power = contract(source, target).astype(BF16)
        least = col_id.astype(F32)
        for turn in range(7):
            least = jnp.minimum(least, contract(power, least.astype(BF16)))
            if turn < 6:
                power = contract(power, power).astype(BF16)
        other = contract(source, least.astype(BF16))
        color_col = color_col * 2 + jnp.where(least > other, 1, 0)
        color_row = jnp.transpose(color_col)

    def lookup(key, value):
        return jnp.sum(jnp.where(key == row_id, value, 0), axis=0, keepdims=True)

    table_ref[...] = jnp.zeros_like(table_ref)
    table_ref[0:1, :] = lookup((col_id & -8) + color_col, col_id & 7)
    table_ref[1:2, :] = lookup(color_col * OWNERS + (final_col >> 3), col_id >> 3)
    table_ref[2:3, :] = lookup(final_col, color_col)


def routing_tables(dest):
    outs = [shaped((8, REQUESTS), jnp.int32)]
    return run_kernel(plan_kernel, [(dest, "h")], outs, "plan_states", flops=2 * 10**9)[0]


LAST = 24
PIECES = 15
MESSAGE = LAST + PIECES * SLOTS
SPARE = 3
def place_pieces(value):
    parts = []
    rest = value
    for _ in range(2):
        high = rest.astype(BF16)
        parts.append(high)
        rest = rest - high.astype(F32)
    parts.append(rest.astype(BF16))
    total = jnp.zeros((SLOTS, 128), F32)
    for piece in range(3):
        spot = hot(iota((8, 128), 1) == iota((8, 128), 0) + 8 * piece)
        total = total + contract(parts[piece], spot)
    return total


def join_pieces(block):
    spot = hot((iota((128, 8), 0) % 8 == iota((128, 8), 1)) & (iota((128, 8), 0) < 24))
    return contract(block.astype(BF16), spot)


def read_rows(pack_ref, first):
    return jnp.concatenate([pack_ref[:, first + piece, :] for piece in range(4)], axis=1)


def sender_match(dest_row, me):
    slot = iota((SLOTS, REQUESTS), 0) + me * SLOTS
    owner = hot((iota((REQUESTS, OWNERS), 0) >> 3) == iota((REQUESTS, OWNERS), 1))
    return contract(hot(jnp.broadcast_to(dest_row, slot.shape) == slot), owner).astype(BF16)


def step_pieces(ins, step):
    x_ref, z_ref, residual_ref, b_ref, c_ref, dt_ref = ins
    columns = pl.ds(pl.multiple_of(lax.axis_index("head") * WIDTH, WIDTH), WIDTH)
    wide = [x_ref[step], z_ref[step], residual_ref[step, :, columns]]
    cut = [value[:, 128 * i : 128 * (i + 1)] for value in wide for i in range(4)]
    return cut + [b_ref[step], c_ref[step], place_pieces(dt_ref[step]).astype(BF16)]


def pack_few_kernel(ins, outs, scratch, wait):
    dest_ref, ids_ref = ins[0], ins[7]
    (message_ref, most_ref), (wide_ref,) = outs, scratch
    me = lax.axis_index("req")
    back = sender_match(dest_ref[0:1, :], me)
    square = (REQUESTS, REQUESTS)
    hop = hot(jnp.broadcast_to(dest_ref[0:1, :], square) == iota(square, 0))
    second = jnp.broadcast_to(dest_ref[1:2, :], (8, REQUESTS)).astype(F32).astype(BF16)
    both = contract(second, hop)[0:1, :].astype(jnp.int32)
    home = sender_match(both, me).astype(F32)
    same = contract(home.astype(BF16), home.astype(BF16), ((1,), (1,)))
    before = iota((SLOTS, SLOTS), 1) < iota((SLOTS, SLOTS), 0)
    rank = jnp.sum(jnp.where(before, same, 0.0), axis=1, keepdims=True)
    target = hot((jnp.broadcast_to(both, (OWNERS, REQUESTS)) >> 3) == iota((OWNERS, REQUESTS), 0))
    source = hot((iota((REQUESTS, OWNERS), 0) >> 3) == iota((REQUESTS, OWNERS), 1))
    most_ref[0, 0] = jnp.max(contract(target, source)).astype(jnp.int32)
    over = ((0,), (0,))
    one = jnp.concatenate(step_pieces(ins[1:7], 1), axis=1)
    two = jnp.concatenate(step_pieces(ins[1:7], 2), axis=1)
    rows = [contract(back, one, over)]
    for place in range(SPARE):
        rows.append(contract(jnp.where(rank == place, home, 0.0).astype(BF16), two, over))
    for block, value in enumerate(rows):
        for row in range(PIECES):
            wide_ref[:, block * 16 + row, :] = value[:, row * 128 : (row + 1) * 128]
    for half in range(2):
        total = jnp.zeros((8, 128), F32)
        for step in range(STEPS):
            for slot in range(4):
                spot = hot(iota((8, 128), 1) == iota((8, 128), 0) + 24 * slot + 8 * step)
                here = ids_ref[step].astype(F32)[half * 4 + slot : half * 4 + slot + 1, :]
                total = total + contract(jnp.broadcast_to(here, (8, 8)).astype(BF16), spot)
        wide_ref[:, half * 16 + 15, :] = jnp.broadcast_to(total[0:1, :], (OWNERS, 128))
    for block in range(2, SPARE + 1):
        wide_ref[:, block * 16 + 15, :] = jnp.zeros((OWNERS, 128), F32)
    message_ref[...] = wide_ref[...].astype(BF16)


def pack_few(*arrays):
    shape = (OWNERS, 16 * (SPARE + 1), 128)
    outs = [shaped(shape, BF16), shaped((1, 1), jnp.int32)]
    scratch = [pltpu.VMEM(shape, F32)]
    args = [(array, "h") for array in arrays]
    specs = [VMEM_SPEC, pl.BlockSpec(memory_space=pltpu.SMEM)]
    return run_kernel(pack_few_kernel, args, outs, "pack_few", scratch, out_specs=specs, limit=58)


def own_slots(dest_ref):
    first = lax.axis_index("req") * SLOTS
    middle = [dest_ref[0, first + slot] for slot in range(SLOTS)]
    return middle, [dest_ref[1, slot] for slot in middle]


def take_few_kernel(ins, outs, scratch, wait):
    dest_ref, got_ref = ins
    (rows_ref, ids_ref), (wide_ref,) = outs, scratch
    middle, final = own_slots(dest_ref)
    for slot in range(SLOTS):
        rows_ref[slot, 0:16, :] = got_ref[middle[slot] // SLOTS, 0:16, :]
        owner = final[slot] // SLOTS
        rank = jnp.int32(0)
        for other in range(SLOTS):
            if other != slot:
                ahead = (final[other] // SLOTS == owner) & (final[other] < final[slot])
                rank = rank + ahead.astype(jnp.int32)
        start = pl.multiple_of(16 + 16 * jnp.minimum(rank, SPARE - 1), 16)
        rows_ref[slot, 16:32, :] = got_ref[owner, pl.ds(start, 16), :]
    wide = got_ref[:, 0:32, :].astype(F32)
    for slot in range(SLOTS):
        row = wide[:, 16 * (slot // 4) + 15, :].astype(BF16)
        lane = iota((128, 128), 1)
        spot = hot((iota((128, 128), 0) == lane - 24 + 24 * (slot % 4)) & (lane >= 24) & (lane < 48))
        wide_ref[:, slot, :] = contract(row, spot)
    ids_ref[...] = wide_ref[...].reshape(REQUESTS, 128).astype(BF16)


def take_all_kernel(ins, outs, scratch, wait):
    dest_ref, got_ref = ins
    (rows_ref, ids_ref), (wide_ref, picked_ref) = outs, scratch
    middle, final = own_slots(dest_ref)
    picked_ref[...] = jnp.zeros_like(picked_ref)
    for slot in range(SLOTS):
        rows_ref[slot, 0:16, :] = got_ref[middle[slot] // SLOTS, 0:16, :]
        wide_ref[slot] = got_ref[final[slot] // SLOTS].astype(F32)
        picked_ref[slot, 0:PIECES, :] = wide_ref[
            slot, pl.ds(LAST + final[slot] % SLOTS, PIECES, stride=SLOTS), :
        ]
    rows_ref[:, 16:32, :] = picked_ref[...].astype(BF16)
    ids = got_ref[:, MESSAGE - 16 :, :].astype(F32)[:, SLOTS:, :]
    ids_ref[...] = ids.reshape(REQUESTS, 128).astype(BF16)


def take(body, dest, got, scratch):
    outs = [shaped((SLOTS, 32, 128), BF16), shaped((REQUESTS, 128), BF16)]
    return tuple(run_kernel(body, [(dest, "s"), (got, "v")], outs, "take_rows", scratch))


def pack_all_kernel(ins, outs, scratch, wait):
    dest_ref, ids_ref = ins[0], ins[7]
    (message_ref,), (wide_ref, last_ref) = outs, scratch
    back = sender_match(dest_ref[0:1, :], lax.axis_index("req"))
    one = step_pieces(ins[1:7], 1)
    two = step_pieces(ins[1:7], 2)
    wide_ref[:, PIECES:LAST, :] = jnp.zeros((OWNERS, LAST - PIECES, 128), F32)
    for row in range(PIECES):
        wide_ref[:, row, :] = contract(back, one[row], ((0,), (0,)))
    ids = jnp.zeros((SLOTS, 128), F32)
    for step in range(STEPS):
        spot = hot(iota((8, 128), 1) == iota((8, 128), 0) + 8 * (step + 3))
        ids = ids + contract(ids_ref[step].astype(F32).astype(BF16), spot)
    wide_ref[:, LAST:32, :] = jnp.broadcast_to(two[0].astype(F32)[None], (OWNERS, SLOTS, 128))
    for row in range(1, PIECES):
        value = two[row].astype(F32)
        if row == PIECES - 1:
            value = value + ids
        last_ref[(row - 1) * SLOTS : row * SLOTS, :] = value
    message_ref[:, 0:32, :] = wide_ref[...].astype(BF16)
    last = last_ref[...].astype(BF16)
    message_ref[:, 32:MESSAGE, :] = jnp.broadcast_to(last[None], (OWNERS,) + last.shape)


def pack_all(*arrays):
    outs = [shaped((OWNERS, MESSAGE, 128), BF16)]
    scratch = [pltpu.VMEM((OWNERS, 32, 128), F32), pltpu.VMEM((MESSAGE - 32, 128), F32)]
    return run_kernel(pack_all_kernel, [(array, "h") for array in arrays], outs, "pack_all", scratch, limit=58)[0]


def head_spread():
    return hot(iota((HEADS, WIDTH), 1) // HSIZE == iota((HEADS, WIDTH), 0))


def widen(value, spread):
    parts = []
    rest = value
    for _ in range(3):
        high = rest.astype(BF16)
        parts.append(high)
        rest = rest - high.astype(F32)
    return contract(parts[0], spread) + contract(parts[1], spread) + contract(parts[2], spread)


def softplus(value):
    return jnp.maximum(value, 0.0) + jnp.log1p(jnp.exp(-jnp.abs(value)))


def mamba_kernel(ins, outs, scratch, wait):
    got_ref, state_ref, x_ref, z_ref, residual_ref, b_ref, c_ref, dt_ref = ins[:8]
    decay_ref, skip_ref, gain_ref, weight_ref = ins[8:]
    keep_ref, send_ref, residual_out_ref, outer_ref, kept_ref, b_rows_ref = outs
    rows_in_ref, c_rows_ref, read_ref, rows_ref = scratch
    column = lax.axis_index("head")
    rows_in_ref[...] = got_ref[...].astype(F32)
    xs = [x_ref[0].astype(F32), read_rows(rows_in_ref, 0), read_rows(rows_in_ref, 16)]
    zs = [z_ref[0].astype(F32), read_rows(rows_in_ref, 4), read_rows(rows_in_ref, 20)]
    steps_b = [b_ref[0].astype(F32), rows_in_ref[:, 12, :], rows_in_ref[:, 28, :]]
    steps_c = [c_ref[0].astype(F32), rows_in_ref[:, 13, :], rows_in_ref[:, 29, :]]
    raws = [dt_ref[0], join_pieces(rows_in_ref[:, 14, :]), join_pieces(rows_in_ref[:, 30, :])]
    own_columns = pl.ds(pl.multiple_of(column * WIDTH, WIDTH), WIDTH)
    residual_out_ref[0:8, :] = residual_ref[0, :, own_columns].astype(F32)
    residual_out_ref[8:16, :] = read_rows(rows_in_ref, 8)
    residual_out_ref[16:24, :] = read_rows(rows_in_ref, 24)

    c_rows_ref[...] = jnp.zeros_like(c_rows_ref)
    for step in range(STEPS):
        c_rows_ref[:, step, :] = steps_c[step]
    across = ((1,), (1,))
    wait(1)
    for slot in range(SLOTS):
        high, low = split_pair(state_ref[slot])
        c_rows = c_rows_ref[slot].astype(BF16)
        read_ref[slot] = contract(c_rows, high, across) + contract(c_rows, low, across)
    spread = head_spread()
    skip = widen(jnp.broadcast_to(skip_ref[...], (SLOTS, HEADS)), spread)
    inputs, kept = [], []
    for step in range(STEPS):
        step_size = softplus(raws[step])
        kept.append(widen(jnp.exp(-decay_ref[...] * step_size), spread))
        inputs.append(widen(step_size, spread) * xs[step])
    for step in range(STEPS):
        total = read_ref[:, step, :] * kept[0]
        for earlier in range(step + 1):
            if earlier > 0:
                total = total * kept[earlier]
            match = jnp.sum(steps_b[earlier] * steps_c[step], axis=1, keepdims=True)
            total = total + inputs[earlier] * match
        gated = (total + skip * xs[step]) * silu(zs[step])
        scale = lax.rsqrt(jnp.mean(gated * gated, axis=1, keepdims=True) + NORM_EPS)
        rows_ref[step * SLOTS : (step + 1) * SLOTS, :] = gated * scale * gain_ref[...]
    rows = rows_ref[...].astype(BF16)
    wait(11)
    for turn in range(HEADS):
        block = 2 * ((column // 2 + turn) % 4) + (column + turn // 4) % 2
        columns = pl.ds(pl.multiple_of(block * WIDTH, WIDTH), WIDTH)
        terms = contract(rows, weight_ref[:, columns]).astype(BF16)
        if turn < 4:
            keep_ref[turn] = terms
        else:
            send_ref[turn - 4] = terms
    late = kept[2]
    factors = [inputs[0] * (kept[1] * late), inputs[1] * late, inputs[2]]
    outer_ref[...] = jnp.zeros_like(outer_ref)
    kept_ref[...] = jnp.zeros_like(kept_ref)
    b_rows_ref[...] = jnp.zeros_like(b_rows_ref)
    for step in range(STEPS):
        outer_ref[:, step, :] = factors[step]
        b_rows_ref[:, step, :] = steps_b[step]
    kept_ref[:, 0, :] = kept[0] * (kept[1] * late)


def mamba(got, state, *arrays):
    part = shaped((4, ROWS, WIDTH), BF16)
    factor = shaped((SLOTS, 8, WIDTH), F32)
    outs = [part, part, shaped((ROWS, WIDTH), F32), factor, factor, shaped((SLOTS, 8, NSTATE), F32)]
    scratch = [
        pltpu.VMEM((SLOTS, 32, 128), F32),
        pltpu.VMEM((SLOTS, 8, NSTATE), F32),
        pltpu.VMEM((SLOTS, 8, WIDTH), F32),
        pltpu.VMEM((ROWS, WIDTH), F32),
    ]
    args = [(got, "v"), (state, "l")] + [(array, "h") for array in arrays[:-1]] + [(arrays[-1], "l")]
    return run_kernel(mamba_kernel, args, outs, "mamba_steps", scratch, 2 * 24 * 512 * 4096, 8 * 2**20, limit=54)


def update_kernel(ins, outs, scratch, wait):
    table_ref, state_any, outer_ref, keep_ref, b_ref = ins
    (out_any,), (state_ref, made_ref, in_sems, out_sems) = outs, scratch
    first = lax.axis_index("req") * SLOTS
    sources = [table_ref[0, first + block] for block in range(SLOTS)]
    loads = [
        pltpu.make_async_copy(state_any.at[sources[block]], state_ref.at[block], in_sems.at[block])
        for block in range(SLOTS)
    ]
    for load in loads:
        load.start()
    stores = []
    ones = jnp.ones((8, NSTATE), BF16)
    along = ((0,), (0,))
    for block in range(SLOTS):
        b_rows = b_ref[sources[block]].astype(BF16)
        outer_high, outer_low = split_pair(outer_ref[sources[block]])
        keep_high, keep_low = split_pair(keep_ref[sources[block]])
        keep = contract(keep_high, ones, along) + contract(keep_low, ones, along)
        added = contract(outer_high, b_rows, along) + contract(outer_low, b_rows, along)
        loads[block].wait()
        made_ref[block] = (keep * state_ref[block] + added).astype(BF16)
        store = pltpu.make_async_copy(made_ref.at[block], out_any.at[block], out_sems.at[block])
        store.start()
        stores.append(store)
    for store in stores:
        store.wait()


def update_states(table, state, factors):
    scratch = [
        pltpu.VMEM(state.shape, F32),
        pltpu.VMEM(state.shape, BF16),
        pltpu.SemaphoreType.DMA((SLOTS,)),
        pltpu.SemaphoreType.DMA((SLOTS,)),
    ]
    args = [(table, "s"), (state, "m")] + [(factor, "h") for factor in factors]
    return run_kernel(
        update_kernel, args, [shaped(state.shape, BF16)], "update_states", scratch,
        2 * 32 * 512 * 1024, 3 * 2**20, [HBM_SPEC],
    )[0]


CORES = [(i, i ^ 1) for i in range(HEADS)]


def along_y(value, distance):
    moves = [(i, ((i // 2 + distance) % 4) * 2 + i % 2) for i in range(HEADS)]
    return lax.ppermute(value, "head", moves)


def add_kernel(tail, ins, outs, scratch, wait):
    keep_ref, got_ref = ins
    first_ref, *rest_refs = outs
    for turn in range(4):
        total = keep_ref[turn].astype(F32) + got_ref[turn].astype(F32)
        if turn == 0:
            first_ref[...] = total
            continue
        out_ref = rest_refs[turn - 1]
        if tail:
            out_ref[:, : 2 * FFE] = total[:, : 2 * FFE].astype(BF16)
            out_ref[:, 2 * FFE :] = pair_lanes(jnp.sum(total[:, 2 * FFE :], axis=1, keepdims=True))
        else:
            out_ref[...] = total.astype(BF16)


def pair_lanes(value):
    high, low = split_pair(value)
    shape = (value.shape[0], 128)
    lane = iota(shape, 1)
    high_wide = jnp.broadcast_to(high.astype(F32), shape)
    low_wide = jnp.broadcast_to(low.astype(F32), shape)
    return jnp.where(lane == 0, high_wide, jnp.where(lane == 1, low_wide, 0.0)).astype(BF16)


def add_cores(keep, got, tail):
    shape = keep.shape[1:]
    outs = [shaped(shape, F32)] + [shaped(shape, BF16)] * 3
    return run_kernel(
        functools.partial(add_kernel, tail), [(keep, "v"), (got, "v")], outs, "add_cores", moved=4 * keep.size
    )


def scatter_sum(keep, send, tail, beside=None):
    got = lax.ppermute(send, "head", CORES)
    first, *rest = add_cores(keep, got, tail)
    if beside is not None:
        first, beside, *rest = lax.optimization_barrier((first, beside, *rest))
        beside = exchange(beside)
    far = along_y(rest[1], 2)
    near = along_y(rest[0], 1)
    other = along_y(rest[2], 3)
    return (first, near, far, other), beside


def stream_kernel(ins, outs, scratch, wait):
    first_ref, a_ref, b_ref, c_ref, residual_ref = ins
    (out_ref,) = outs
    total = first_ref[...] + a_ref[...].astype(F32) + b_ref[...].astype(F32) + c_ref[...].astype(F32)
    stream = (residual_ref[...] + total).astype(BF16)
    out_ref[...] = jnp.broadcast_to(stream[None], out_ref.shape)


def stream_copies(parts, residual):
    args = [(part, "v") for part in parts] + [(residual, "v")]
    return run_kernel(stream_kernel, args, [shaped((OWNERS, ROWS, WIDTH), BF16)], "stream_copies")[0]


def routes_kernel(ins, outs, scratch, wait):
    dest_ref, all_ids_ref, ids_ref, weights_ref = ins
    pick_ref, kept_ref, high_ref, low_ref = outs
    me = lax.axis_index("req")
    column = lax.axis_index("head")
    total_rows = OWNERS * ROWS
    square = (REQUESTS, REQUESTS)
    row_id = iota(square, 1)
    col_id = iota(square, 0)
    first = dest_ref[0:1, :]
    second = jnp.broadcast_to(dest_ref[1:2, :], (8, REQUESTS)).astype(F32).astype(BF16)
    hop_one = hot(jnp.broadcast_to(first, square) == col_id)
    both = contract(second, hop_one)[0:1, :].astype(jnp.int32)
    hops = [hot(row_id == col_id), hop_one, hot(jnp.broadcast_to(both, square) == col_id)]
    slots = [iota((1, REQUESTS), 1), first, both]
    spread = []
    for step in range(STEPS):
        shape = (REQUESTS, total_rows)
        g = iota(shape, 0)
        spread.append(hot(iota(shape, 1) == (g >> 3) * ROWS + step * SLOTS + (g & 7)))
    at_row = jnp.zeros((8, total_rows), F32)
    for step in range(STEPS):
        wide = jnp.broadcast_to(slots[step], (8, REQUESTS)).astype(F32).astype(BF16)
        at_row = at_row + contract(wide, spread[step])
    ids = all_ids_ref[...].astype(F32)
    step_of = hot((iota((128, 128), 0) >> 3) == iota((128, 128), 1) + 3)
    earlier = hot(((row_id >> 3) == (col_id >> 3)) & (row_id < col_id))
    slot = iota((REQUESTS, 128), 0)
    lane = iota((REQUESTS, 128), 1)
    owner = slot >> 3
    part = owner >> 2
    turn = (((part & 1) + column) & 1) * 4 + (((part >> 1) - (column >> 1)) & 3)
    base = turn * (CHUNK // 2) + (owner & 3) * (STEPS * CAP) + lane * CAP
    for expert in range(2):
        match = (ids == (me * 2 + expert).astype(F32)) & (lane >= 24) & (lane < 48)
        named = contract(hot(match), step_of)
        rank = contract(earlier, named.astype(BF16))
        target = jnp.where(named > 0.5, base.astype(F32) + rank + 1.0, 0.0).astype(BF16)
        row = jnp.zeros((8, total_rows), F32)
        for step in range(STEPS):
            select = hot(iota((8, 128), 1) == step)
            by_slot = contract(select, target, ((1,), (1,)))
            by_home = contract(by_slot.astype(BF16), hops[step])
            row = row + contract(by_home.astype(BF16), spread[step])
        half = OWNERS * STEPS * CAP
        want = iota((half, total_rows), 0).astype(F32) + 1.0
        pick_ref[expert * half : (expert + 1) * half, :] = hot(jnp.broadcast_to(row[0:1, :], (half, total_rows)) == want)
    shape = (ROWS, total_rows)
    mine = (me * SLOTS + iota(shape, 0) % SLOTS).astype(F32)
    step_match = (iota(shape, 1) % ROWS) // SLOTS == iota(shape, 0) // SLOTS
    kept_ref[...] = hot((jnp.broadcast_to(at_row[0:1, :], shape) == mine) & step_match)
    expert_lane = iota((ROWS, 128), 1)
    chosen = jnp.zeros((ROWS, 128), F32)
    weight = jnp.zeros((ROWS, 128), F32)
    for choice in range(8):
        hit = expert_lane == ids_ref[:, choice : choice + 1]
        chosen = chosen + jnp.where(hit, 1.0, 0.0)
        weight = weight + jnp.where(hit, weights_ref[:, choice : choice + 1], 0.0)
    small = (ROWS, ROWS)
    before = hot((iota(small, 0) // SLOTS == iota(small, 1) // SLOTS) & (iota(small, 1) < iota(small, 0)))
    rank = contract(before, chosen.astype(BF16))
    span = OWNERS * CHUNK
    place = iota((128, span), 1) % CHUNK % 12
    expert_of = 2 * (iota((128, span), 1) // CHUNK) + place // 6
    to_place = hot(iota((128, span), 0) == expert_of)
    spot = iota((ROWS, span), 1) % CHUNK
    fits = (contract(rank.astype(BF16), to_place) == (spot % 2).astype(F32)) & (
        (spot % 6) // 2 == iota((ROWS, span), 0) // SLOTS
    )
    for value, out_ref in zip(split_pair(weight), (high_ref, low_ref)):
        value = jnp.where(fits, contract(value, to_place), 0.0)
        for piece in range(4):
            out_ref[piece] = jnp.where(spot // 12 == piece, value, 0.0).astype(BF16)


def routes(dest, all_ids, ids, weights):
    total_rows = OWNERS * ROWS
    mixing = shaped((4, ROWS, OWNERS * CHUNK), BF16)
    outs = [
        shaped((2 * OWNERS * STEPS * CAP, total_rows), BF16),
        shaped((ROWS, total_rows), BF16),
        mixing,
        mixing,
    ]
    args = [(dest, "h"), (all_ids, "v"), (ids, "h"), (weights, "h")]
    return run_kernel(routes_kernel, args, outs, "routes", flops=10**9)


def expand_kernel(ins, outs, scratch, wait):
    pick_ref, stream_ref, gain_ref, gate_ref, up_ref = ins
    keep_ref, send_ref = outs
    half = pick_ref.shape[0] // 2
    some = CHUNK // 2
    for expert in range(2):
        picked = contract(pick_ref[expert * half : (expert + 1) * half, :], stream_ref[...])
        tail = pair_lanes(jnp.sum(picked * picked, axis=1, keepdims=True))
        scaled = (picked * gain_ref[...]).astype(BF16)
        if expert == 0:
            wait(3)
            wait(4)
        values = [
            contract(scaled, gate_ref[expert]).astype(BF16),
            contract(scaled, up_ref[expert]).astype(BF16),
            tail,
        ]
        rows = slice(expert * some, (expert + 1) * some)
        for turn in range(HEADS):
            out_ref = keep_ref if turn < 4 else send_ref
            source = slice(turn * some, (turn + 1) * some)
            for value, start in zip(values, (0, FFE, 2 * FFE)):
                out_ref[turn % 4, rows, start : start + value.shape[1]] = value[source, :]


def expand(pick, stream, gain, gate_weight, up_weight):
    part = shaped((4, CHUNK, TERMS), BF16)
    args = [(pick, "h"), (stream, "v"), (gain, "h"), (gate_weight, "l"), (up_weight, "l")]
    return run_kernel(
        expand_kernel, args, [part, part], "expand_experts", flops=2 * 384 * 512 * (2048 + 768), moved=8 * 2**20
    )


def hidden_kernel(ins, outs, scratch, wait):
    first_ref, a_ref, b_ref, c_ref = ins
    (out_ref,) = outs
    total = first_ref[...] + a_ref[...].astype(F32) + b_ref[...].astype(F32) + c_ref[...].astype(F32)
    square = jnp.sum(total[:, 2 * FFE :], axis=1, keepdims=True)
    inverse = lax.rsqrt(square * (1.0 / (HEADS * WIDTH)) + NORM_EPS)
    out_ref[...] = (silu(total[:, :FFE] * inverse) * (total[:, FFE : 2 * FFE] * inverse)).astype(BF16)


def hidden_units(parts):
    args = [(part, "v") for part in parts]
    return run_kernel(hidden_kernel, args, [shaped((CHUNK, FFE), BF16)], "hidden_units")[0]


def shrink_kernel(ins, outs, scratch, wait):
    table_ref, pieces_ref, weight_ref, *hidden_refs = ins
    (out_ref,), (sems,) = outs, scratch
    first = lax.axis_index("req") // 4 * OWNERS
    column = lax.axis_index("head")
    moves = [
        pltpu.make_async_copy(
            pieces_ref.at[table_ref[1, first + block]],
            out_ref.at[block, pl.ds(CHUNK, 2 * HSIZE), :],
            sems.at[block],
        )
        for block in range(OWNERS)
    ]
    for move in moves:
        move.start()
    hidden = jnp.concatenate([ref[...] for ref in hidden_refs], axis=0)
    wait(2)
    served = [contract(hidden, weight_ref[expert]) for expert in range(2)]
    shape = (4 * 16, CHUNK)
    row, source = iota(shape, 0), iota(shape, 1)
    inside = row % 16
    spot = hot((inside < 12) & (source == (inside // 6) * (CHUNK // 2) + (row // 16) * 6 + inside % 6))
    half = iota((CHUNK, WIDTH), 0) < CHUNK // 2
    for turn in range(HEADS):
        rows = slice(turn * CHUNK, (turn + 1) * CHUNK)
        chunk = jnp.where(half, served[0][rows], served[1][rows]).astype(BF16)
        owner = (2 * ((column // 2 - turn + 8) % 4) + (column + turn // 4) % 2) * 4
        block = contract(spot, chunk)
        for piece in range(4):
            wide = block[piece * 16 : piece * 16 + 12, :]
            cut = [wide[:, 128 * i : 128 * (i + 1)] for i in range(4)]
            out_ref[owner + piece, 0:CHUNK, :] = jnp.concatenate(cut, axis=0).astype(BF16)
    for move in moves:
        move.wait()


def shrink(table, pieces, hidden, weight):
    args = [(table, "s"), (pieces, "m"), (weight, "l")] + [(block, "v") for block in hidden]
    outs = [shaped((OWNERS, CHUNK + 2 * HSIZE, 128), BF16)]
    return run_kernel(
        shrink_kernel, args, outs, "shrink_experts", [pltpu.SemaphoreType.DMA((OWNERS,))],
        2 * 2 * 384 * 1024 * 512, 4 * 2**20,
    )[0]


def finish_kernel(ins, outs, scratch, wait):
    table_ref, back_ref, high_ref, low_ref, kept_ref, stream_ref = ins
    mixed_ref, states_any = outs
    made_ref, sems = scratch
    first = lax.axis_index("req") * SLOTS
    stores = []
    for slot in range(SLOTS):
        color = table_ref[2, first + slot]
        for piece in range(4):
            rows = slice(piece * 2 * HSIZE, (piece + 1) * 2 * HSIZE)
            made_ref[slot, rows, :] = back_ref[color * 4 + piece, CHUNK:, :].astype(F32)
        store = pltpu.make_async_copy(made_ref.at[slot], states_any.at[slot], sems.at[slot])
        store.start()
        stores.append(store)
    served = back_ref[:, 0:CHUNK, :].reshape(OWNERS * CHUNK, 128)
    for ref in (2, 3, 4, 5):
        wait(ref)
    stream = contract(kept_ref[...], stream_ref[...])
    for piece in range(4):
        columns = slice(piece * 128, (piece + 1) * 128)
        mixed = contract(high_ref[piece], served) + contract(low_ref[piece], served)
        mixed_ref[:, columns] = (stream[:, columns] + mixed).astype(BF16)
    for store in stores:
        store.wait()


def finish(table, back, high, low, kept, streams):
    args = [(table, "s"), (back, "v"), (high, "l"), (low, "l"), (kept, "l"), (streams, "l")]
    outs = [shaped((ROWS, WIDTH), BF16), shaped((SLOTS, HEADS * HSIZE, NSTATE), F32)]
    scratch = [pltpu.VMEM((SLOTS, HEADS * HSIZE, NSTATE), F32), pltpu.SemaphoreType.DMA((SLOTS,))]
    return run_kernel(
        finish_kernel, args, outs, "finish", scratch, 10**8, 4 * 2**20, [VMEM_SPEC, HBM_SPEC]
    )


def exchange(value):
    return lax.all_to_all(value, "req", split_axis=0, concat_axis=0, tiled=True)


def shards(
    states, ssm_x, gate_z, ssm_b, ssm_c, dt_raw, decay_rate, skip_gain, ssm_gain, out_weight,
    residual, ffn_gain, route_ids, route_weights, gate_weight, up_weight, down_weight, dest,
):
    fence = lax.optimization_barrier
    state_rows = states.reshape(SLOTS, HEADS * HSIZE, NSTATE)
    own = (ssm_x, gate_z, residual, ssm_b, ssm_c, dt_raw)

    message, most = pack_few(dest, *own, route_ids)

    def few(message):
        scratch = [pltpu.VMEM((OWNERS, SLOTS, 128), F32)]
        return take(take_few_kernel, dest, exchange(message), scratch)

    def every(_):
        scratch = [pltpu.VMEM((SLOTS, MESSAGE, 128), F32), pltpu.VMEM((SLOTS, 16, 128), F32)]
        return take(take_all_kernel, dest, exchange(pack_all(dest, *own, route_ids)), scratch)

    rows, all_ids = lax.cond(most[0, 0] <= SPARE, few, every, message)

    keep_part, send_part, home_residual, *factors = mamba(
        rows, state_rows, *own, decay_rate[None], skip_gain[None], ssm_gain[None], out_weight
    )
    parts, _ = scatter_sum(keep_part, send_part, False)
    copies, later_dest, all_ids, factors = fence((stream_copies(parts, home_residual), dest, all_ids, factors))
    streams = exchange(copies).reshape(OWNERS * ROWS, WIDTH)
    table = routing_tables(later_dest)
    routed = routes(later_dest, all_ids, route_ids.reshape(ROWS, 8), route_weights.reshape(ROWS, 8))
    pieces = update_states(table, state_rows, factors)
    streams, pieces, (pick, kept, high, low) = fence((streams, pieces, routed))

    keep_part, send_part = expand(pick, streams, ffn_gain[None], gate_weight, up_weight)
    parts, pieces = scatter_sum(keep_part, send_part, True, pieces.reshape(OWNERS, 2 * HSIZE, NSTATE))
    hidden = hidden_units(parts)
    far = along_y(hidden, 2)
    near = along_y(hidden, 1)
    other = along_y(hidden, 3)
    blocks = [hidden, near, far, other]
    blocks = blocks + [lax.ppermute(block, "head", CORES) for block in blocks]
    back = exchange(shrink(table, pieces, blocks, down_weight))
    mixed, final_states = finish(table, back, high, low, kept, streams)
    return mixed.reshape(STEPS, SLOTS, WIDTH), final_states.reshape(states.shape)


def solution(mesh):
    placed = (
        P("req", "head", None, None),
        P(None, "req", "head"),
        P(None, "req", "head"),
        P(None, "req", "head"),
        P(None, "req", "head"),
        P(None, "req", "head"),
        P("head"),
        P("head"),
        P("head"),
        P("head", None),
        P(None, "req", None),
        P("head"),
        P(None, "req", None),
        P(None, "req", None),
        P("req", "head", None),
        P("req", "head", None),
        P("req", None, "head"),
        P(),
    )
    return jax.shard_map(
        shards,
        mesh=mesh,
        in_specs=placed,
        out_specs=(P(None, "req", "head"), P("req", "head", None, None)),
        check_vma=False,
    )
```

```python
import functools

import jax
import jax.numpy as jnp
from jax import lax
from jax.experimental import pallas as pl
from jax.experimental.pallas import tpu as pltpu
from jax.sharding import PartitionSpec as P

NSTATE = 128
EXPERTS = 64
STEPS = 3
CAP = 2
OWNERS = 32
SLOTS = 8
REQUESTS = OWNERS * SLOTS
HEADS = 8
HSIZE = 64
WIDTH = 512
FFE = 1024
ROWS = STEPS * SLOTS
TERMS = 2 * FFE + 128
CHUNK = 48
NORM_EPS = 1e-05
F32 = jnp.float32
BF16 = jnp.bfloat16
VMEM_SPEC = pl.BlockSpec(memory_space=pltpu.VMEM)
HBM_SPEC = pl.BlockSpec(memory_space=pltpu.HBM)


def params(mebibytes):
    return pltpu.CompilerParams(vmem_limit_bytes=mebibytes * 2**20)


def cost(flops, moved):
    return pl.CostEstimate(flops=flops, bytes_accessed=moved, transcendentals=0)


def run_kernel(body, args, outs, name, scratch=(), flops=0, moved=2**20, out_specs=None, limit=24):
    count, made = len(args), len(outs)
    modes = [mode for _, mode in args]
    copied = [i for i, mode in enumerate(modes) if mode in "hls"]

    def kernel(*refs):
        ins = list(refs[:count])
        results = refs[count : count + made]
        rest = refs[count + made :]
        copies = {}
        for position, i in enumerate(copied):
            copies[i] = pltpu.make_async_copy(ins[i], rest[position], rest[len(copied)].at[position])
            ins[i] = rest[position]
        for copy in copies.values():
            copy.start()
        for i, copy in copies.items():
            if modes[i] != "l":
                copy.wait()
        own = rest[len(copied) + 1 :] if copied else rest
        body(ins, results, own, lambda i: copies[i].wait())

    spaces = [(pltpu.SMEM if modes[i] == "s" else pltpu.VMEM)(args[i][0].shape, args[i][0].dtype) for i in copied]
    if copied:
        spaces.append(pltpu.SemaphoreType.DMA((len(copied),)))
    return pl.pallas_call(
        kernel,
        out_shape=tuple(outs),
        in_specs=[VMEM_SPEC if mode == "v" else HBM_SPEC for mode in modes],
        out_specs=tuple(out_specs or [VMEM_SPEC] * made),
        scratch_shapes=spaces + list(scratch),
        compiler_params=params(limit),
        cost_estimate=cost(flops, moved),
        name=name,
    )(*[array for array, _ in args])


def shaped(shape, dtype):
    return jax.ShapeDtypeStruct(shape, dtype)


def split_pair(value):
    high = value.astype(BF16)
    low = (value - high.astype(F32)).astype(BF16)
    return high, low


def contract(a, b, dims=((1,), (0,))):
    return lax.dot_general(a, b, (dims, ((), ())), preferred_element_type=F32)


def iota(shape, dim):
    return lax.broadcasted_iota(jnp.int32, shape, dim)


def hot(condition):
    return jnp.where(condition, 1.0, 0.0).astype(BF16)


def silu(value):
    return value / (1.0 + jnp.exp(-value))


def plan_kernel(ins, outs, scratch, wait):
    (dest_ref,), (table_ref,) = ins, outs
    size = (REQUESTS, REQUESTS)
    row_id = iota(size, 1)
    col_id = iota(size, 0)
    first_row = jnp.broadcast_to(dest_ref[0:1, :], size)
    second_row = jnp.broadcast_to(dest_ref[1:2, :], size)
    first_col = jnp.transpose(first_row)
    second_col = jnp.transpose(second_row).astype(F32).astype(BF16)
    final_col = contract(hot(first_col == row_id), second_col).astype(jnp.int32)
    final_row = jnp.transpose(final_col)
    differs = row_id != col_id
    color_col = jnp.zeros(size, jnp.int32)
    color_row = color_col
    for level in (1, 2, 3):
        alike = (color_col == color_row) & differs
        source = hot(((row_id >> level) == (col_id >> level)) & alike)
        target = hot(((final_row >> level) == (final_col >> level)) & alike)
        power = contract(source, target).astype(BF16)
        least = col_id.astype(F32)
        for turn in range(7):
            least = jnp.minimum(least, contract(power, least.astype(BF16)))
            if turn < 6:
                power = contract(power, power).astype(BF16)
        other = contract(source, least.astype(BF16))
        color_col = color_col * 2 + jnp.where(least > other, 1, 0)
        color_row = jnp.transpose(color_col)

    def lookup(key, value):
        return jnp.sum(jnp.where(key == row_id, value, 0), axis=0, keepdims=True)

    table_ref[...] = jnp.zeros_like(table_ref)
    table_ref[0:1, :] = lookup((col_id & -8) + color_col, col_id & 7)
    table_ref[1:2, :] = lookup(color_col * OWNERS + (final_col >> 3), col_id >> 3)
    table_ref[2:3, :] = lookup(final_col, color_col)


def routing_tables(dest):
    outs = [shaped((8, REQUESTS), jnp.int32)]
    return run_kernel(plan_kernel, [(dest, "h")], outs, "plan_states", flops=2 * 10**9)[0]


LAST = 24
PIECES = 15
MESSAGE = LAST + PIECES * SLOTS
SPARE = 3
def place_pieces(value):
    parts = []
    rest = value
    for _ in range(2):
        high = rest.astype(BF16)
        parts.append(high)
        rest = rest - high.astype(F32)
    parts.append(rest.astype(BF16))
    total = jnp.zeros((SLOTS, 128), F32)
    for piece in range(3):
        spot = hot(iota((8, 128), 1) == iota((8, 128), 0) + 8 * piece)
        total = total + contract(parts[piece], spot)
    return total


def join_pieces(block):
    spot = hot((iota((128, 8), 0) % 8 == iota((128, 8), 1)) & (iota((128, 8), 0) < 24))
    return contract(block.astype(BF16), spot)


def read_rows(pack_ref, first):
    return jnp.concatenate([pack_ref[:, first + piece, :] for piece in range(4)], axis=1)


def sender_match(dest_row, me):
    slot = iota((SLOTS, REQUESTS), 0) + me * SLOTS
    owner = hot((iota((REQUESTS, OWNERS), 0) >> 3) == iota((REQUESTS, OWNERS), 1))
    return contract(hot(jnp.broadcast_to(dest_row, slot.shape) == slot), owner).astype(BF16)


def step_pieces(ins, step):
    x_ref, z_ref, residual_ref, b_ref, c_ref, dt_ref = ins
    columns = pl.ds(pl.multiple_of(lax.axis_index("head") * WIDTH, WIDTH), WIDTH)
    wide = [x_ref[step], z_ref[step], residual_ref[step, :, columns]]
    cut = [value[:, 128 * i : 128 * (i + 1)] for value in wide for i in range(4)]
    return cut + [b_ref[step], c_ref[step], place_pieces(dt_ref[step]).astype(BF16)]


def pack_few_kernel(ins, outs, scratch, wait):
    dest_ref, ids_ref = ins[0], ins[7]
    (message_ref, most_ref), (wide_ref,) = outs, scratch
    me = lax.axis_index("req")
    back = sender_match(dest_ref[0:1, :], me)
    square = (REQUESTS, REQUESTS)
    hop = hot(jnp.broadcast_to(dest_ref[0:1, :], square) == iota(square, 0))
    second = jnp.broadcast_to(dest_ref[1:2, :], (8, REQUESTS)).astype(F32).astype(BF16)
    both = contract(second, hop)[0:1, :].astype(jnp.int32)
    home = sender_match(both, me).astype(F32)
    same = contract(home.astype(BF16), home.astype(BF16), ((1,), (1,)))
    before = iota((SLOTS, SLOTS), 1) < iota((SLOTS, SLOTS), 0)
    rank = jnp.sum(jnp.where(before, same, 0.0), axis=1, keepdims=True)
    target = hot((jnp.broadcast_to(both, (OWNERS, REQUESTS)) >> 3) == iota((OWNERS, REQUESTS), 0))
    source = hot((iota((REQUESTS, OWNERS), 0) >> 3) == iota((REQUESTS, OWNERS), 1))
    most_ref[0, 0] = jnp.max(contract(target, source)).astype(jnp.int32)
    over = ((0,), (0,))
    one = jnp.concatenate(step_pieces(ins[1:7], 1), axis=1)
    two = jnp.concatenate(step_pieces(ins[1:7], 2), axis=1)
    rows = [contract(back, one, over)]
    for place in range(SPARE):
        rows.append(contract(jnp.where(rank == place, home, 0.0).astype(BF16), two, over))
    for block, value in enumerate(rows):
        for row in range(PIECES):
            wide_ref[:, block * 16 + row, :] = value[:, row * 128 : (row + 1) * 128]
    for half in range(2):
        total = jnp.zeros((8, 128), F32)
        for step in range(STEPS):
            for slot in range(4):
                spot = hot(iota((8, 128), 1) == iota((8, 128), 0) + 24 * slot + 8 * step)
                here = ids_ref[step].astype(F32)[half * 4 + slot : half * 4 + slot + 1, :]
                total = total + contract(jnp.broadcast_to(here, (8, 8)).astype(BF16), spot)
        wide_ref[:, half * 16 + 15, :] = jnp.broadcast_to(total[0:1, :], (OWNERS, 128))
    for block in range(2, SPARE + 1):
        wide_ref[:, block * 16 + 15, :] = jnp.zeros((OWNERS, 128), F32)
    message_ref[...] = wide_ref[...].astype(BF16)


def pack_few(*arrays):
    shape = (OWNERS, 16 * (SPARE + 1), 128)
    outs = [shaped(shape, BF16), shaped((1, 1), jnp.int32)]
    scratch = [pltpu.VMEM(shape, F32)]
    args = [(array, "h") for array in arrays]
    specs = [VMEM_SPEC, pl.BlockSpec(memory_space=pltpu.SMEM)]
    return run_kernel(pack_few_kernel, args, outs, "pack_few", scratch, out_specs=specs, limit=58)


def own_slots(dest_ref):
    first = lax.axis_index("req") * SLOTS
    middle = [dest_ref[0, first + slot] for slot in range(SLOTS)]
    return middle, [dest_ref[1, slot] for slot in middle]


def take_few_kernel(ins, outs, scratch, wait):
    dest_ref, got_ref = ins
    (rows_ref, ids_ref), (wide_ref,) = outs, scratch
    middle, final = own_slots(dest_ref)
    for slot in range(SLOTS):
        rows_ref[slot, 0:16, :] = got_ref[middle[slot] // SLOTS, 0:16, :]
        owner = final[slot] // SLOTS
        rank = jnp.int32(0)
        for other in range(SLOTS):
            if other != slot:
                ahead = (final[other] // SLOTS == owner) & (final[other] < final[slot])
                rank = rank + ahead.astype(jnp.int32)
        start = pl.multiple_of(16 + 16 * jnp.minimum(rank, SPARE - 1), 16)
        rows_ref[slot, 16:32, :] = got_ref[owner, pl.ds(start, 16), :]
    wide = got_ref[:, 0:32, :].astype(F32)
    for slot in range(SLOTS):
        row = wide[:, 16 * (slot // 4) + 15, :].astype(BF16)
        lane = iota((128, 128), 1)
        spot = hot((iota((128, 128), 0) == lane - 24 + 24 * (slot % 4)) & (lane >= 24) & (lane < 48))
        wide_ref[:, slot, :] = contract(row, spot)
    ids_ref[...] = wide_ref[...].reshape(REQUESTS, 128).astype(BF16)


def take_all_kernel(ins, outs, scratch, wait):
    dest_ref, got_ref = ins
    (rows_ref, ids_ref), (wide_ref, picked_ref) = outs, scratch
    middle, final = own_slots(dest_ref)
    picked_ref[...] = jnp.zeros_like(picked_ref)
    for slot in range(SLOTS):
        rows_ref[slot, 0:16, :] = got_ref[middle[slot] // SLOTS, 0:16, :]
        wide_ref[slot] = got_ref[final[slot] // SLOTS].astype(F32)
        picked_ref[slot, 0:PIECES, :] = wide_ref[
            slot, pl.ds(LAST + final[slot] % SLOTS, PIECES, stride=SLOTS), :
        ]
    rows_ref[:, 16:32, :] = picked_ref[...].astype(BF16)
    ids = got_ref[:, MESSAGE - 16 :, :].astype(F32)[:, SLOTS:, :]
    ids_ref[...] = ids.reshape(REQUESTS, 128).astype(BF16)


def take(body, dest, got, scratch):
    outs = [shaped((SLOTS, 32, 128), BF16), shaped((REQUESTS, 128), BF16)]
    return tuple(run_kernel(body, [(dest, "s"), (got, "v")], outs, "take_rows", scratch))


def pack_all_kernel(ins, outs, scratch, wait):
    dest_ref, ids_ref = ins[0], ins[7]
    (message_ref,), (wide_ref, last_ref) = outs, scratch
    back = sender_match(dest_ref[0:1, :], lax.axis_index("req"))
    one = step_pieces(ins[1:7], 1)
    two = step_pieces(ins[1:7], 2)
    wide_ref[:, PIECES:LAST, :] = jnp.zeros((OWNERS, LAST - PIECES, 128), F32)
    for row in range(PIECES):
        wide_ref[:, row, :] = contract(back, one[row], ((0,), (0,)))
    ids = jnp.zeros((SLOTS, 128), F32)
    for step in range(STEPS):
        spot = hot(iota((8, 128), 1) == iota((8, 128), 0) + 8 * (step + 3))
        ids = ids + contract(ids_ref[step].astype(F32).astype(BF16), spot)
    wide_ref[:, LAST:32, :] = jnp.broadcast_to(two[0].astype(F32)[None], (OWNERS, SLOTS, 128))
    for row in range(1, PIECES):
        value = two[row].astype(F32)
        if row == PIECES - 1:
            value = value + ids
        last_ref[(row - 1) * SLOTS : row * SLOTS, :] = value
    message_ref[:, 0:32, :] = wide_ref[...].astype(BF16)
    last = last_ref[...].astype(BF16)
    message_ref[:, 32:MESSAGE, :] = jnp.broadcast_to(last[None], (OWNERS,) + last.shape)


def pack_all(*arrays):
    outs = [shaped((OWNERS, MESSAGE, 128), BF16)]
    scratch = [pltpu.VMEM((OWNERS, 32, 128), F32), pltpu.VMEM((MESSAGE - 32, 128), F32)]
    return run_kernel(pack_all_kernel, [(array, "h") for array in arrays], outs, "pack_all", scratch, limit=58)[0]


def head_spread():
    return hot(iota((HEADS, WIDTH), 1) // HSIZE == iota((HEADS, WIDTH), 0))


def widen(value, spread):
    parts = []
    rest = value
    for _ in range(3):
        high = rest.astype(BF16)
        parts.append(high)
        rest = rest - high.astype(F32)
    return contract(parts[0], spread) + contract(parts[1], spread) + contract(parts[2], spread)


def softplus(value):
    return jnp.maximum(value, 0.0) + jnp.log1p(jnp.exp(-jnp.abs(value)))


def mamba_kernel(ins, outs, scratch, wait):
    got_ref, state_ref, x_ref, z_ref, residual_ref, b_ref, c_ref, dt_ref = ins[:8]
    decay_ref, skip_ref, gain_ref, weight_ref = ins[8:]
    keep_ref, send_ref, residual_out_ref, outer_ref, kept_ref, b_rows_ref = outs
    rows_in_ref, c_rows_ref, read_ref, rows_ref = scratch
    column = lax.axis_index("head")
    rows_in_ref[...] = got_ref[...].astype(F32)
    xs = [x_ref[0].astype(F32), read_rows(rows_in_ref, 0), read_rows(rows_in_ref, 16)]
    zs = [z_ref[0].astype(F32), read_rows(rows_in_ref, 4), read_rows(rows_in_ref, 20)]
    steps_b = [b_ref[0].astype(F32), rows_in_ref[:, 12, :], rows_in_ref[:, 28, :]]
    steps_c = [c_ref[0].astype(F32), rows_in_ref[:, 13, :], rows_in_ref[:, 29, :]]
    raws = [dt_ref[0], join_pieces(rows_in_ref[:, 14, :]), join_pieces(rows_in_ref[:, 30, :])]
    own_columns = pl.ds(pl.multiple_of(column * WIDTH, WIDTH), WIDTH)
    residual_out_ref[0:8, :] = residual_ref[0, :, own_columns].astype(F32)
    residual_out_ref[8:16, :] = read_rows(rows_in_ref, 8)
    residual_out_ref[16:24, :] = read_rows(rows_in_ref, 24)

    c_rows_ref[...] = jnp.zeros_like(c_rows_ref)
    for step in range(STEPS):
        c_rows_ref[:, step, :] = steps_c[step]
    across = ((1,), (1,))
    wait(1)
    for slot in range(SLOTS):
        high, low = split_pair(state_ref[slot])
        c_rows = c_rows_ref[slot].astype(BF16)
        read_ref[slot] = contract(c_rows, high, across) + contract(c_rows, low, across)
    spread = head_spread()
    skip = widen(jnp.broadcast_to(skip_ref[...], (SLOTS, HEADS)), spread)
    inputs, kept = [], []
    for step in range(STEPS):
        step_size = softplus(raws[step])
        kept.append(widen(jnp.exp(-decay_ref[...] * step_size), spread))
        inputs.append(widen(step_size, spread) * xs[step])
    for step in range(STEPS):
        total = read_ref[:, step, :] * kept[0]
        for earlier in range(step + 1):
            if earlier > 0:
                total = total * kept[earlier]
            match = jnp.sum(steps_b[earlier] * steps_c[step], axis=1, keepdims=True)
            total = total + inputs[earlier] * match
        gated = (total + skip * xs[step]) * silu(zs[step])
        scale = lax.rsqrt(jnp.mean(gated * gated, axis=1, keepdims=True) + NORM_EPS)
        rows_ref[step * SLOTS : (step + 1) * SLOTS, :] = gated * scale * gain_ref[...]
    rows = rows_ref[...].astype(BF16)
    wait(11)
    for turn in range(HEADS):
        block = 2 * ((column // 2 + turn) % 4) + (column + turn // 4) % 2
        columns = pl.ds(pl.multiple_of(block * WIDTH, WIDTH), WIDTH)
        terms = contract(rows, weight_ref[:, columns]).astype(BF16)
        if turn < 4:
            keep_ref[turn] = terms
        else:
            send_ref[turn - 4] = terms
    late = kept[2]
    factors = [inputs[0] * (kept[1] * late), inputs[1] * late, inputs[2]]
    outer_ref[...] = jnp.zeros_like(outer_ref)
    kept_ref[...] = jnp.zeros_like(kept_ref)
    b_rows_ref[...] = jnp.zeros_like(b_rows_ref)
    for step in range(STEPS):
        outer_ref[:, step, :] = factors[step]
        b_rows_ref[:, step, :] = steps_b[step]
    kept_ref[:, 0, :] = kept[0] * (kept[1] * late)


def mamba(got, state, *arrays):
    part = shaped((4, ROWS, WIDTH), BF16)
    factor = shaped((SLOTS, 8, WIDTH), F32)
    outs = [part, part, shaped((ROWS, WIDTH), F32), factor, factor, shaped((SLOTS, 8, NSTATE), F32)]
    scratch = [
        pltpu.VMEM((SLOTS, 32, 128), F32),
        pltpu.VMEM((SLOTS, 8, NSTATE), F32),
        pltpu.VMEM((SLOTS, 8, WIDTH), F32),
        pltpu.VMEM((ROWS, WIDTH), F32),
    ]
    args = [(got, "v"), (state, "l")] + [(array, "h") for array in arrays[:-1]] + [(arrays[-1], "l")]
    return run_kernel(mamba_kernel, args, outs, "mamba_steps", scratch, 2 * 24 * 512 * 4096, 8 * 2**20, limit=50)


def update_kernel(ins, outs, scratch, wait):
    table_ref, state_any, outer_ref, keep_ref, b_ref = ins
    (out_any,), (state_ref, made_ref, in_sems, out_sems) = outs, scratch
    first = lax.axis_index("req") * SLOTS
    sources = [table_ref[0, first + block] for block in range(SLOTS)]
    loads = [
        pltpu.make_async_copy(state_any.at[sources[block]], state_ref.at[block], in_sems.at[block])
        for block in range(SLOTS)
    ]
    for load in loads:
        load.start()
    stores = []
    ones = jnp.ones((8, NSTATE), BF16)
    along = ((0,), (0,))
    for block in range(SLOTS):
        b_rows = b_ref[sources[block]].astype(BF16)
        outer_high, outer_low = split_pair(outer_ref[sources[block]])
        keep_high, keep_low = split_pair(keep_ref[sources[block]])
        keep = contract(keep_high, ones, along) + contract(keep_low, ones, along)
        added = contract(outer_high, b_rows, along) + contract(outer_low, b_rows, along)
        loads[block].wait()
        made_ref[block] = (keep * state_ref[block] + added).astype(BF16)
        store = pltpu.make_async_copy(made_ref.at[block], out_any.at[block], out_sems.at[block])
        store.start()
        stores.append(store)
    for store in stores:
        store.wait()


def update_states(table, state, factors):
    scratch = [
        pltpu.VMEM(state.shape, F32),
        pltpu.VMEM(state.shape, BF16),
        pltpu.SemaphoreType.DMA((SLOTS,)),
        pltpu.SemaphoreType.DMA((SLOTS,)),
    ]
    args = [(table, "s"), (state, "m")] + [(factor, "h") for factor in factors]
    return run_kernel(
        update_kernel, args, [shaped(state.shape, BF16)], "update_states", scratch,
        2 * 32 * 512 * 1024, 3 * 2**20, [HBM_SPEC],
    )[0]


CORES = [(i, i ^ 1) for i in range(HEADS)]


LINE = 8
LINES = OWNERS // LINE


def along_x(value, distance):
    moves = [(i, ((i // LINE + distance) % LINES) * LINE + i % LINE) for i in range(OWNERS)]
    return lax.ppermute(value, "req", moves)


def along_y(value, distance):
    moves = [(i, ((i // 2 + distance) % 4) * 2 + i % 2) for i in range(HEADS)]
    return lax.ppermute(value, "head", moves)


def add_kernel(tail, ins, outs, scratch, wait):
    keep_ref, got_ref = ins
    first_ref, *rest_refs = outs
    for turn in range(4):
        total = keep_ref[turn].astype(F32) + got_ref[turn].astype(F32)
        if turn == 0:
            first_ref[...] = total
            continue
        out_ref = rest_refs[turn - 1]
        if tail:
            out_ref[:, : 2 * FFE] = total[:, : 2 * FFE].astype(BF16)
            out_ref[:, 2 * FFE :] = pair_lanes(jnp.sum(total[:, 2 * FFE :], axis=1, keepdims=True))
        else:
            out_ref[...] = total.astype(BF16)


def pair_lanes(value):
    high, low = split_pair(value)
    shape = (value.shape[0], 128)
    lane = iota(shape, 1)
    high_wide = jnp.broadcast_to(high.astype(F32), shape)
    low_wide = jnp.broadcast_to(low.astype(F32), shape)
    return jnp.where(lane == 0, high_wide, jnp.where(lane == 1, low_wide, 0.0)).astype(BF16)


def add_cores(keep, got, tail):
    shape = keep.shape[1:]
    outs = [shaped(shape, F32)] + [shaped(shape, BF16)] * 3
    return run_kernel(
        functools.partial(add_kernel, tail), [(keep, "v"), (got, "v")], outs, "add_cores", moved=4 * keep.size
    )


def scatter_sum(keep, send, tail, beside=None):
    got = lax.ppermute(send, "head", CORES)
    first, *rest = add_cores(keep, got, tail)
    if beside is not None:
        first, beside, *rest = lax.optimization_barrier((first, beside, *rest))
        beside = exchange(beside)
    far = along_y(rest[1], 2)
    near = along_y(rest[0], 1)
    other = along_y(rest[2], 3)
    return (first, near, far, other), beside


def stream_kernel(ins, outs, scratch, wait):
    first_ref, a_ref, b_ref, c_ref, residual_ref = ins
    (out_ref,) = outs
    total = first_ref[...] + a_ref[...].astype(F32) + b_ref[...].astype(F32) + c_ref[...].astype(F32)
    stream = (residual_ref[...] + total).astype(BF16)
    out_ref[...] = jnp.broadcast_to(stream[None], out_ref.shape)


def stream_copies(parts, residual):
    args = [(part, "v") for part in parts] + [(residual, "v")]
    return run_kernel(stream_kernel, args, [shaped((LINE, ROWS, WIDTH), BF16)], "stream_copies")[0]


def routes_kernel(ins, outs, scratch, wait):
    dest_ref, all_ids_ref, ids_ref, weights_ref = ins
    pick_ref, kept_ref, high_ref, low_ref = outs
    me = lax.axis_index("req")
    column = lax.axis_index("head")
    total_rows = OWNERS * ROWS
    square = (REQUESTS, REQUESTS)
    row_id = iota(square, 1)
    col_id = iota(square, 0)
    first = dest_ref[0:1, :]
    second = jnp.broadcast_to(dest_ref[1:2, :], (8, REQUESTS)).astype(F32).astype(BF16)
    hop_one = hot(jnp.broadcast_to(first, square) == col_id)
    both = contract(second, hop_one)[0:1, :].astype(jnp.int32)
    hops = [hot(row_id == col_id), hop_one, hot(jnp.broadcast_to(both, square) == col_id)]
    slots = [iota((1, REQUESTS), 1), first, both]
    spread = []
    for step in range(STEPS):
        shape = (REQUESTS, total_rows)
        g = iota(shape, 0)
        source = (((me >> 3) - (g >> 6)) & 3) * LINE + ((g >> 3) & 7)
        spread.append(hot(iota(shape, 1) == source * ROWS + step * SLOTS + (g & 7)))
    at_row = jnp.zeros((8, total_rows), F32)
    for step in range(STEPS):
        wide = jnp.broadcast_to(slots[step], (8, REQUESTS)).astype(F32).astype(BF16)
        at_row = at_row + contract(wide, spread[step])
    ids = all_ids_ref[...].astype(F32)
    step_of = hot((iota((128, 128), 0) >> 3) == iota((128, 128), 1) + 3)
    earlier = hot(((row_id >> 3) == (col_id >> 3)) & (row_id < col_id))
    slot = iota((REQUESTS, 128), 0)
    lane = iota((REQUESTS, 128), 1)
    owner = slot >> 3
    part = owner >> 2
    turn = (((part & 1) + column) & 1) * 4 + (((part >> 1) - (column >> 1)) & 3)
    base = turn * (CHUNK // 2) + (owner & 3) * (STEPS * CAP) + lane * CAP
    for expert in range(2):
        match = (ids == (me * 2 + expert).astype(F32)) & (lane >= 24) & (lane < 48)
        named = contract(hot(match), step_of)
        rank = contract(earlier, named.astype(BF16))
        target = jnp.where(named > 0.5, base.astype(F32) + rank + 1.0, 0.0).astype(BF16)
        row = jnp.zeros((8, total_rows), F32)
        for step in range(STEPS):
            select = hot(iota((8, 128), 1) == step)
            by_slot = contract(select, target, ((1,), (1,)))
            by_home = contract(by_slot.astype(BF16), hops[step])
            row = row + contract(by_home.astype(BF16), spread[step])
        half = OWNERS * STEPS * CAP
        want = iota((half, total_rows), 0).astype(F32) + 1.0
        pick_ref[expert * half : (expert + 1) * half, :] = hot(jnp.broadcast_to(row[0:1, :], (half, total_rows)) == want)
    shape = (ROWS, total_rows)
    mine = (me * SLOTS + iota(shape, 0) % SLOTS).astype(F32)
    step_match = (iota(shape, 1) % ROWS) // SLOTS == iota(shape, 0) // SLOTS
    kept_ref[...] = hot((jnp.broadcast_to(at_row[0:1, :], shape) == mine) & step_match)
    expert_lane = iota((ROWS, 128), 1)
    chosen = jnp.zeros((ROWS, 128), F32)
    weight = jnp.zeros((ROWS, 128), F32)
    for choice in range(8):
        hit = expert_lane == ids_ref[:, choice : choice + 1]
        chosen = chosen + jnp.where(hit, 1.0, 0.0)
        weight = weight + jnp.where(hit, weights_ref[:, choice : choice + 1], 0.0)
    small = (ROWS, ROWS)
    before = hot((iota(small, 0) // SLOTS == iota(small, 1) // SLOTS) & (iota(small, 1) < iota(small, 0)))
    rank = contract(before, chosen.astype(BF16))
    span = OWNERS * CHUNK
    place = iota((128, span), 1) % CHUNK % 12
    expert_of = 2 * (iota((128, span), 1) // CHUNK) + place // 6
    to_place = hot(iota((128, span), 0) == expert_of)
    spot = iota((ROWS, span), 1) % CHUNK
    fits = (contract(rank.astype(BF16), to_place) == (spot % 2).astype(F32)) & (
        (spot % 6) // 2 == iota((ROWS, span), 0) // SLOTS
    )
    for value, out_ref in zip(split_pair(weight), (high_ref, low_ref)):
        out_ref[...] = jnp.where(fits, contract(value, to_place), 0.0).astype(BF16)


def routes(dest, all_ids, ids, weights):
    total_rows = OWNERS * ROWS
    mixing = shaped((ROWS, OWNERS * CHUNK), BF16)
    outs = [
        shaped((2 * OWNERS * STEPS * CAP, total_rows), BF16),
        shaped((ROWS, total_rows), BF16),
        mixing,
        mixing,
    ]
    args = [(dest, "h"), (all_ids, "v"), (ids, "h"), (weights, "h")]
    return run_kernel(routes_kernel, args, outs, "routes", flops=10**9)


def expand_kernel(ins, outs, scratch, wait):
    pick_ref, kept_ref, *stream_refs, gain_ref, gate_ref, up_ref = ins
    keep_ref, send_ref, own_ref = outs

    def choose(rows):
        total = 0.0
        for line, ref in enumerate(stream_refs):
            total = total + contract(rows[:, line * LINE * ROWS : (line + 1) * LINE * ROWS], ref[...])
        return total

    own_ref[...] = choose(kept_ref[...]).astype(BF16)
    half = pick_ref.shape[0] // 2
    some = CHUNK // 2
    for expert in range(2):
        picked = choose(pick_ref[expert * half : (expert + 1) * half, :])
        tail = pair_lanes(jnp.sum(picked * picked, axis=1, keepdims=True))
        scaled = (picked * gain_ref[...]).astype(BF16)
        if expert == 0:
            wait(7)
            wait(8)
        values = [
            contract(scaled, gate_ref[expert]).astype(BF16),
            contract(scaled, up_ref[expert]).astype(BF16),
            tail,
        ]
        rows = slice(expert * some, (expert + 1) * some)
        for turn in range(HEADS):
            out_ref = keep_ref if turn < 4 else send_ref
            source = slice(turn * some, (turn + 1) * some)
            for value, start in zip(values, (0, FFE, 2 * FFE)):
                out_ref[turn % 4, rows, start : start + value.shape[1]] = value[source, :]


def expand(pick, kept, streams, gain, gate_weight, up_weight):
    part = shaped((4, CHUNK, TERMS), BF16)
    args = [(pick, "h"), (kept, "h")] + [(stream, "v") for stream in streams]
    args += [(gain, "h"), (gate_weight, "l"), (up_weight, "l")]
    return run_kernel(
        expand_kernel, args, [part, part, shaped((ROWS, WIDTH), BF16)], "expand_experts", flops=2 * 384 * 512 * (2048 + 768), moved=8 * 2**20
    )


def hidden_kernel(ins, outs, scratch, wait):
    first_ref, a_ref, b_ref, c_ref = ins
    (out_ref,) = outs
    total = first_ref[...] + a_ref[...].astype(F32) + b_ref[...].astype(F32) + c_ref[...].astype(F32)
    square = jnp.sum(total[:, 2 * FFE :], axis=1, keepdims=True)
    inverse = lax.rsqrt(square * (1.0 / (HEADS * WIDTH)) + NORM_EPS)
    out_ref[...] = (silu(total[:, :FFE] * inverse) * (total[:, FFE : 2 * FFE] * inverse)).astype(BF16)


def hidden_units(parts):
    args = [(part, "v") for part in parts]
    return run_kernel(hidden_kernel, args, [shaped((CHUNK, FFE), BF16)], "hidden_units")[0]


def shrink_kernel(ins, outs, scratch, wait):
    table_ref, pieces_ref, weight_ref, *hidden_refs = ins
    (out_ref,), (sems,) = outs, scratch
    first = lax.axis_index("req") // 4 * OWNERS
    column = lax.axis_index("head")
    moves = [
        pltpu.make_async_copy(
            pieces_ref.at[table_ref[1, first + block]],
            out_ref.at[block, pl.ds(CHUNK, 2 * HSIZE), :],
            sems.at[block],
        )
        for block in range(OWNERS)
    ]
    for move in moves:
        move.start()
    hidden = jnp.concatenate([ref[...] for ref in hidden_refs], axis=0)
    wait(2)
    served = [contract(hidden, weight_ref[expert]) for expert in range(2)]
    shape = (4 * 16, CHUNK)
    row, source = iota(shape, 0), iota(shape, 1)
    inside = row % 16
    spot = hot((inside < 12) & (source == (inside // 6) * (CHUNK // 2) + (row // 16) * 6 + inside % 6))
    half = iota((CHUNK, WIDTH), 0) < CHUNK // 2
    for turn in range(HEADS):
        rows = slice(turn * CHUNK, (turn + 1) * CHUNK)
        chunk = jnp.where(half, served[0][rows], served[1][rows]).astype(BF16)
        owner = (2 * ((column // 2 - turn + 8) % 4) + (column + turn // 4) % 2) * 4
        block = contract(spot, chunk)
        for piece in range(4):
            wide = block[piece * 16 : piece * 16 + 12, :]
            cut = [wide[:, 128 * i : 128 * (i + 1)] for i in range(4)]
            out_ref[owner + piece, 0:CHUNK, :] = jnp.concatenate(cut, axis=0).astype(BF16)
    for move in moves:
        move.wait()


def shrink(table, pieces, hidden, weight):
    args = [(table, "s"), (pieces, "m"), (weight, "l")] + [(block, "v") for block in hidden]
    outs = [shaped((OWNERS, CHUNK + 2 * HSIZE, 128), BF16)]
    return run_kernel(
        shrink_kernel, args, outs, "shrink_experts", [pltpu.SemaphoreType.DMA((OWNERS,))],
        2 * 2 * 384 * 1024 * 512, 4 * 2**20, limit=56,
    )[0]


def finish_kernel(ins, outs, scratch, wait):
    table_ref, back_ref, high_ref, low_ref, stream_ref = ins
    mixed_ref, states_any = outs
    made_ref, sems = scratch
    first = lax.axis_index("req") * SLOTS
    stores = []
    for slot in range(SLOTS):
        color = table_ref[2, first + slot]
        for piece in range(4):
            rows = slice(piece * 2 * HSIZE, (piece + 1) * 2 * HSIZE)
            made_ref[slot, rows, :] = back_ref[color * 4 + piece, CHUNK:, :].astype(F32)
        store = pltpu.make_async_copy(made_ref.at[slot], states_any.at[slot], sems.at[slot])
        store.start()
        stores.append(store)
    served = back_ref[:, 0:CHUNK, :].reshape(OWNERS * CHUNK, 128)
    for ref in (2, 3, 4):
        wait(ref)
    stream = stream_ref[...].astype(F32)
    high, low = high_ref[...].astype(F32), low_ref[...].astype(F32)
    for piece in range(4):
        columns = slice(piece * 128, (piece + 1) * 128)
        here = iota((ROWS, OWNERS * CHUNK), 1) % CHUNK // 12 == piece
        mixed = contract(jnp.where(here, high, 0.0).astype(BF16), served)
        mixed = mixed + contract(jnp.where(here, low, 0.0).astype(BF16), served)
        mixed_ref[:, columns] = (stream[:, columns] + mixed).astype(BF16)
    for store in stores:
        store.wait()


def finish(table, back, high, low, stream):
    args = [(table, "s"), (back, "v"), (high, "l"), (low, "l"), (stream, "l")]
    outs = [shaped((ROWS, WIDTH), BF16), shaped((SLOTS, HEADS * HSIZE, NSTATE), F32)]
    scratch = [pltpu.VMEM((SLOTS, HEADS * HSIZE, NSTATE), F32), pltpu.SemaphoreType.DMA((SLOTS,))]
    return run_kernel(
        finish_kernel, args, outs, "finish", scratch, 10**8, 4 * 2**20, [VMEM_SPEC, HBM_SPEC]
    )


def exchange(value):
    return lax.all_to_all(value, "req", split_axis=0, concat_axis=0, tiled=True)


def shards(
    states, ssm_x, gate_z, ssm_b, ssm_c, dt_raw, decay_rate, skip_gain, ssm_gain, out_weight,
    residual, ffn_gain, route_ids, route_weights, gate_weight, up_weight, down_weight, dest,
):
    fence = lax.optimization_barrier
    state_rows = states.reshape(SLOTS, HEADS * HSIZE, NSTATE)
    own = (ssm_x, gate_z, residual, ssm_b, ssm_c, dt_raw)

    message, most = pack_few(dest, *own, route_ids)

    def few(message):
        scratch = [pltpu.VMEM((OWNERS, SLOTS, 128), F32)]
        got, table = fence((exchange(message), routing_tables(dest)))
        return take(take_few_kernel, dest, got, scratch) + (table,)

    def every(_):
        scratch = [pltpu.VMEM((SLOTS, MESSAGE, 128), F32), pltpu.VMEM((SLOTS, 16, 128), F32)]
        got, table = fence((exchange(pack_all(dest, *own, route_ids)), routing_tables(dest)))
        return take(take_all_kernel, dest, got, scratch) + (table,)

    rows, all_ids, table = lax.cond(most[0, 0] <= SPARE, few, every, message)

    keep_part, send_part, home_residual, *factors = mamba(
        rows, state_rows, *own, decay_rate[None], skip_gain[None], ssm_gain[None], out_weight
    )
    parts, _ = scatter_sum(keep_part, send_part, False)
    copies, later_dest, all_ids, factors = fence((stream_copies(parts, home_residual), dest, all_ids, factors))
    lines = [[line * LINE + place for place in range(LINE)] for line in range(LINES)]
    line = lax.all_to_all(
        copies, "req", split_axis=0, concat_axis=0, axis_index_groups=lines, tiled=True
    ).reshape(LINE * ROWS, WIDTH)
    streams = [line, along_x(line, 1), along_x(line, 2), along_x(line, 3)]
    routed = routes(later_dest, all_ids, route_ids.reshape(ROWS, 8), route_weights.reshape(ROWS, 8))
    pieces = update_states(table, state_rows, factors)
    streams, pieces, (pick, kept, high, low) = fence((streams, pieces, routed))

    keep_part, send_part, own_stream = expand(pick, kept, streams, ffn_gain[None], gate_weight, up_weight)
    parts, pieces = scatter_sum(keep_part, send_part, True, pieces.reshape(OWNERS, 2 * HSIZE, NSTATE))
    hidden = hidden_units(parts)
    far = along_y(hidden, 2)
    near = along_y(hidden, 1)
    other = along_y(hidden, 3)
    blocks = [hidden, near, far, other]
    blocks = blocks + [lax.ppermute(block, "head", CORES) for block in blocks]
    back = exchange(shrink(table, pieces, blocks, down_weight))
    mixed, final_states = finish(table, back, high, low, own_stream)
    return mixed.reshape(STEPS, SLOTS, WIDTH), final_states.reshape(states.shape)


def solution(mesh):
    placed = (
        P("req", "head", None, None),
        P(None, "req", "head"),
        P(None, "req", "head"),
        P(None, "req", "head"),
        P(None, "req", "head"),
        P(None, "req", "head"),
        P("head"),
        P("head"),
        P("head"),
        P("head", None),
        P(None, "req", None),
        P("head"),
        P(None, "req", None),
        P(None, "req", None),
        P("req", "head", None),
        P("req", "head", None),
        P("req", None, "head"),
        P(),
    )
    return jax.shard_map(
        shards,
        mesh=mesh,
        in_specs=placed,
        out_specs=(P(None, "req", "head"), P("req", "head", None, None)),
        check_vma=False,
    )
```

```python
import functools

import jax
import jax.numpy as jnp
from jax import lax
from jax.experimental import pallas as pl
from jax.experimental.pallas import tpu as pltpu
from jax.sharding import PartitionSpec as P

NSTATE = 128
EXPERTS = 64
STEPS = 3
CAP = 2
OWNERS = 32
SLOTS = 8
REQUESTS = OWNERS * SLOTS
HEADS = 8
HSIZE = 64
WIDTH = 512
FFE = 1024
ROWS = STEPS * SLOTS
TERMS = 2 * FFE + 128
CHUNK = 48
NORM_EPS = 1e-05
F32 = jnp.float32
BF16 = jnp.bfloat16
VMEM_SPEC = pl.BlockSpec(memory_space=pltpu.VMEM)
HBM_SPEC = pl.BlockSpec(memory_space=pltpu.HBM)


def params(mebibytes):
    return pltpu.CompilerParams(vmem_limit_bytes=mebibytes * 2**20)


def cost(flops, moved):
    return pl.CostEstimate(flops=flops, bytes_accessed=moved, transcendentals=0)


def run_kernel(body, args, outs, name, scratch=(), flops=0, moved=2**20, out_specs=None, limit=24):
    count, made = len(args), len(outs)
    modes = [mode for _, mode in args]
    copied = [i for i, mode in enumerate(modes) if mode in "hls"]

    def kernel(*refs):
        ins = list(refs[:count])
        results = refs[count : count + made]
        rest = refs[count + made :]
        copies = {}
        for position, i in enumerate(copied):
            copies[i] = pltpu.make_async_copy(ins[i], rest[position], rest[len(copied)].at[position])
            ins[i] = rest[position]
        for copy in copies.values():
            copy.start()
        for i, copy in copies.items():
            if modes[i] != "l":
                copy.wait()
        own = rest[len(copied) + 1 :] if copied else rest
        body(ins, results, own, lambda i: copies[i].wait())

    spaces = [(pltpu.SMEM if modes[i] == "s" else pltpu.VMEM)(args[i][0].shape, args[i][0].dtype) for i in copied]
    if copied:
        spaces.append(pltpu.SemaphoreType.DMA((len(copied),)))
    return pl.pallas_call(
        kernel,
        out_shape=tuple(outs),
        in_specs=[VMEM_SPEC if mode == "v" else HBM_SPEC for mode in modes],
        out_specs=tuple(out_specs or [VMEM_SPEC] * made),
        scratch_shapes=spaces + list(scratch),
        compiler_params=params(limit),
        cost_estimate=cost(flops, moved),
        name=name,
    )(*[array for array, _ in args])


def shaped(shape, dtype):
    return jax.ShapeDtypeStruct(shape, dtype)


def split_pair(value):
    high = value.astype(BF16)
    low = (value - high.astype(F32)).astype(BF16)
    return high, low


def contract(a, b, dims=((1,), (0,))):
    return lax.dot_general(a, b, (dims, ((), ())), preferred_element_type=F32)


def iota(shape, dim):
    return lax.broadcasted_iota(jnp.int32, shape, dim)


def hot(condition):
    return jnp.where(condition, 1.0, 0.0).astype(BF16)


def silu(value):
    return value / (1.0 + jnp.exp(-value))


def plan_kernel(ins, outs, scratch, wait):
    (dest_ref,), (table_ref,) = ins, outs
    size = (REQUESTS, REQUESTS)
    row_id = iota(size, 1)
    col_id = iota(size, 0)
    first_row = jnp.broadcast_to(dest_ref[0:1, :], size)
    second_row = jnp.broadcast_to(dest_ref[1:2, :], size)
    first_col = jnp.transpose(first_row)
    second_col = jnp.transpose(second_row).astype(F32).astype(BF16)
    final_col = contract(hot(first_col == row_id), second_col).astype(jnp.int32)
    final_row = jnp.transpose(final_col)
    differs = row_id != col_id
    color_col = jnp.zeros(size, jnp.int32)
    color_row = color_col
    for level in (1, 2, 3):
        alike = (color_col == color_row) & differs
        source = hot(((row_id >> level) == (col_id >> level)) & alike)
        target = hot(((final_row >> level) == (final_col >> level)) & alike)
        power = contract(source, target).astype(BF16)
        least = col_id.astype(F32)
        for turn in range(7):
            least = jnp.minimum(least, contract(power, least.astype(BF16)))
            if turn < 6:
                power = contract(power, power).astype(BF16)
        other = contract(source, least.astype(BF16))
        color_col = color_col * 2 + jnp.where(least > other, 1, 0)
        color_row = jnp.transpose(color_col)

    def lookup(key, value):
        return jnp.sum(jnp.where(key == row_id, value, 0), axis=0, keepdims=True)

    table_ref[...] = jnp.zeros_like(table_ref)
    table_ref[0:1, :] = lookup((col_id & -8) + color_col, col_id & 7)
    table_ref[1:2, :] = lookup(color_col * OWNERS + (final_col >> 3), col_id >> 3)
    table_ref[2:3, :] = lookup(final_col, color_col)


def routing_tables(dest):
    outs = [shaped((8, REQUESTS), jnp.int32)]
    return run_kernel(plan_kernel, [(dest, "h")], outs, "plan_states", flops=2 * 10**9)[0]


LAST = 24
PIECES = 15
MESSAGE = LAST + PIECES * SLOTS
SPARE = 3
def place_pieces(value):
    parts = []
    rest = value
    for _ in range(2):
        high = rest.astype(BF16)
        parts.append(high)
        rest = rest - high.astype(F32)
    parts.append(rest.astype(BF16))
    total = jnp.zeros((SLOTS, 128), F32)
    for piece in range(3):
        spot = hot(iota((8, 128), 1) == iota((8, 128), 0) + 8 * piece)
        total = total + contract(parts[piece], spot)
    return total


def join_pieces(block):
    spot = hot((iota((128, 8), 0) % 8 == iota((128, 8), 1)) & (iota((128, 8), 0) < 24))
    return contract(block.astype(BF16), spot)


def read_rows(pack_ref, first):
    return jnp.concatenate([pack_ref[:, first + piece, :] for piece in range(4)], axis=1)


def sender_match(dest_row, me):
    slot = iota((SLOTS, REQUESTS), 0) + me * SLOTS
    owner = hot((iota((REQUESTS, OWNERS), 0) >> 3) == iota((REQUESTS, OWNERS), 1))
    return contract(hot(jnp.broadcast_to(dest_row, slot.shape) == slot), owner).astype(BF16)


def step_pieces(ins, step):
    x_ref, z_ref, residual_ref, b_ref, c_ref, dt_ref = ins
    columns = pl.ds(pl.multiple_of(lax.axis_index("head") * WIDTH, WIDTH), WIDTH)
    wide = [x_ref[step], z_ref[step], residual_ref[step, :, columns]]
    cut = [value[:, 128 * i : 128 * (i + 1)] for value in wide for i in range(4)]
    return cut + [b_ref[step], c_ref[step], place_pieces(dt_ref[step]).astype(BF16)]


def pack_few_kernel(ins, outs, scratch, wait):
    dest_ref, ids_ref = ins[0], ins[7]
    (message_ref, most_ref), (wide_ref,) = outs, scratch
    me = lax.axis_index("req")
    back = sender_match(dest_ref[0:1, :], me)
    square = (REQUESTS, REQUESTS)
    hop = hot(jnp.broadcast_to(dest_ref[0:1, :], square) == iota(square, 0))
    second = jnp.broadcast_to(dest_ref[1:2, :], (8, REQUESTS)).astype(F32).astype(BF16)
    both = contract(second, hop)[0:1, :].astype(jnp.int32)
    home = sender_match(both, me).astype(F32)
    same = contract(home.astype(BF16), home.astype(BF16), ((1,), (1,)))
    before = iota((SLOTS, SLOTS), 1) < iota((SLOTS, SLOTS), 0)
    rank = jnp.sum(jnp.where(before, same, 0.0), axis=1, keepdims=True)
    target = hot((jnp.broadcast_to(both, (OWNERS, REQUESTS)) >> 3) == iota((OWNERS, REQUESTS), 0))
    source = hot((iota((REQUESTS, OWNERS), 0) >> 3) == iota((REQUESTS, OWNERS), 1))
    most_ref[0, 0] = jnp.max(contract(target, source)).astype(jnp.int32)
    over = ((0,), (0,))
    one = jnp.concatenate(step_pieces(ins[1:7], 1), axis=1)
    two = jnp.concatenate(step_pieces(ins[1:7], 2), axis=1)
    rows = [contract(back, one, over)]
    for place in range(SPARE):
        rows.append(contract(jnp.where(rank == place, home, 0.0).astype(BF16), two, over))
    for block, value in enumerate(rows):
        for row in range(PIECES):
            wide_ref[:, block * 16 + row, :] = value[:, row * 128 : (row + 1) * 128]
    for half in range(2):
        total = jnp.zeros((8, 128), F32)
        for step in range(STEPS):
            for slot in range(4):
                spot = hot(iota((8, 128), 1) == iota((8, 128), 0) + 24 * slot + 8 * step)
                here = ids_ref[step].astype(F32)[half * 4 + slot : half * 4 + slot + 1, :]
                total = total + contract(jnp.broadcast_to(here, (8, 8)).astype(BF16), spot)
        wide_ref[:, half * 16 + 15, :] = jnp.broadcast_to(total[0:1, :], (OWNERS, 128))
    for block in range(2, SPARE + 1):
        wide_ref[:, block * 16 + 15, :] = jnp.zeros((OWNERS, 128), F32)
    message_ref[...] = wide_ref[...].astype(BF16)


def pack_few(*arrays):
    shape = (OWNERS, 16 * (SPARE + 1), 128)
    outs = [shaped(shape, BF16), shaped((1, 1), jnp.int32)]
    scratch = [pltpu.VMEM(shape, F32)]
    args = [(array, "h") for array in arrays]
    specs = [VMEM_SPEC, pl.BlockSpec(memory_space=pltpu.SMEM)]
    return run_kernel(pack_few_kernel, args, outs, "pack_few", scratch, out_specs=specs, limit=58)


def own_slots(dest_ref):
    first = lax.axis_index("req") * SLOTS
    middle = [dest_ref[0, first + slot] for slot in range(SLOTS)]
    return middle, [dest_ref[1, slot] for slot in middle]


def take_few_kernel(ins, outs, scratch, wait):
    dest_ref, got_ref = ins
    (rows_ref, ids_ref), (wide_ref,) = outs, scratch
    middle, final = own_slots(dest_ref)
    for slot in range(SLOTS):
        rows_ref[slot, 0:16, :] = got_ref[middle[slot] // SLOTS, 0:16, :]
        owner = final[slot] // SLOTS
        rank = jnp.int32(0)
        for other in range(SLOTS):
            if other != slot:
                ahead = (final[other] // SLOTS == owner) & (final[other] < final[slot])
                rank = rank + ahead.astype(jnp.int32)
        start = pl.multiple_of(16 + 16 * jnp.minimum(rank, SPARE - 1), 16)
        rows_ref[slot, 16:32, :] = got_ref[owner, pl.ds(start, 16), :]
    wide = got_ref[:, 0:32, :].astype(F32)
    for slot in range(SLOTS):
        row = wide[:, 16 * (slot // 4) + 15, :].astype(BF16)
        lane = iota((128, 128), 1)
        spot = hot((iota((128, 128), 0) == lane - 24 + 24 * (slot % 4)) & (lane >= 24) & (lane < 48))
        wide_ref[:, slot, :] = contract(row, spot)
    ids_ref[...] = wide_ref[...].reshape(REQUESTS, 128).astype(BF16)


def take_all_kernel(ins, outs, scratch, wait):
    dest_ref, got_ref = ins
    (rows_ref, ids_ref), (wide_ref, picked_ref) = outs, scratch
    middle, final = own_slots(dest_ref)
    picked_ref[...] = jnp.zeros_like(picked_ref)
    for slot in range(SLOTS):
        rows_ref[slot, 0:16, :] = got_ref[middle[slot] // SLOTS, 0:16, :]
        wide_ref[slot] = got_ref[final[slot] // SLOTS].astype(F32)
        picked_ref[slot, 0:PIECES, :] = wide_ref[
            slot, pl.ds(LAST + final[slot] % SLOTS, PIECES, stride=SLOTS), :
        ]
    rows_ref[:, 16:32, :] = picked_ref[...].astype(BF16)
    ids = got_ref[:, MESSAGE - 16 :, :].astype(F32)[:, SLOTS:, :]
    ids_ref[...] = ids.reshape(REQUESTS, 128).astype(BF16)


def take(body, dest, got, scratch):
    outs = [shaped((SLOTS, 32, 128), BF16), shaped((REQUESTS, 128), BF16)]
    return tuple(run_kernel(body, [(dest, "s"), (got, "v")], outs, "take_rows", scratch))


def pack_all_kernel(ins, outs, scratch, wait):
    dest_ref, ids_ref = ins[0], ins[7]
    (message_ref,), (wide_ref, last_ref) = outs, scratch
    back = sender_match(dest_ref[0:1, :], lax.axis_index("req"))
    one = step_pieces(ins[1:7], 1)
    two = step_pieces(ins[1:7], 2)
    wide_ref[:, PIECES:LAST, :] = jnp.zeros((OWNERS, LAST - PIECES, 128), F32)
    for row in range(PIECES):
        wide_ref[:, row, :] = contract(back, one[row], ((0,), (0,)))
    ids = jnp.zeros((SLOTS, 128), F32)
    for step in range(STEPS):
        spot = hot(iota((8, 128), 1) == iota((8, 128), 0) + 8 * (step + 3))
        ids = ids + contract(ids_ref[step].astype(F32).astype(BF16), spot)
    wide_ref[:, LAST:32, :] = jnp.broadcast_to(two[0].astype(F32)[None], (OWNERS, SLOTS, 128))
    for row in range(1, PIECES):
        value = two[row].astype(F32)
        if row == PIECES - 1:
            value = value + ids
        last_ref[(row - 1) * SLOTS : row * SLOTS, :] = value
    message_ref[:, 0:32, :] = wide_ref[...].astype(BF16)
    last = last_ref[...].astype(BF16)
    message_ref[:, 32:MESSAGE, :] = jnp.broadcast_to(last[None], (OWNERS,) + last.shape)


def pack_all(*arrays):
    outs = [shaped((OWNERS, MESSAGE, 128), BF16)]
    scratch = [pltpu.VMEM((OWNERS, 32, 128), F32), pltpu.VMEM((MESSAGE - 32, 128), F32)]
    return run_kernel(pack_all_kernel, [(array, "h") for array in arrays], outs, "pack_all", scratch, limit=58)[0]


def head_spread():
    return hot(iota((HEADS, WIDTH), 1) // HSIZE == iota((HEADS, WIDTH), 0))


def widen(value, spread):
    parts = []
    rest = value
    for _ in range(3):
        high = rest.astype(BF16)
        parts.append(high)
        rest = rest - high.astype(F32)
    return contract(parts[0], spread) + contract(parts[1], spread) + contract(parts[2], spread)


def softplus(value):
    return jnp.maximum(value, 0.0) + jnp.log1p(jnp.exp(-jnp.abs(value)))


def mamba_kernel(ins, outs, scratch, wait):
    got_ref, state_ref, x_ref, z_ref, residual_ref, b_ref, c_ref, dt_ref = ins[:8]
    decay_ref, skip_ref, gain_ref, weight_ref = ins[8:]
    keep_ref, send_ref, residual_out_ref, outer_ref, kept_ref, b_rows_ref = outs
    rows_in_ref, c_rows_ref, read_ref, rows_ref = scratch
    column = lax.axis_index("head")
    rows_in_ref[...] = got_ref[...].astype(F32)
    xs = [x_ref[0].astype(F32), read_rows(rows_in_ref, 0), read_rows(rows_in_ref, 16)]
    zs = [z_ref[0].astype(F32), read_rows(rows_in_ref, 4), read_rows(rows_in_ref, 20)]
    steps_b = [b_ref[0].astype(F32), rows_in_ref[:, 12, :], rows_in_ref[:, 28, :]]
    steps_c = [c_ref[0].astype(F32), rows_in_ref[:, 13, :], rows_in_ref[:, 29, :]]
    raws = [dt_ref[0], join_pieces(rows_in_ref[:, 14, :]), join_pieces(rows_in_ref[:, 30, :])]
    own_columns = pl.ds(pl.multiple_of(column * WIDTH, WIDTH), WIDTH)
    residual_out_ref[0:8, :] = residual_ref[0, :, own_columns].astype(F32)
    residual_out_ref[8:16, :] = read_rows(rows_in_ref, 8)
    residual_out_ref[16:24, :] = read_rows(rows_in_ref, 24)

    c_rows_ref[...] = jnp.zeros_like(c_rows_ref)
    for step in range(STEPS):
        c_rows_ref[:, step, :] = steps_c[step]
    across = ((1,), (1,))
    wait(1)
    for slot in range(SLOTS):
        high, low = split_pair(state_ref[slot])
        c_rows = c_rows_ref[slot].astype(BF16)
        read_ref[slot] = contract(c_rows, high, across) + contract(c_rows, low, across)
    spread = head_spread()
    skip = widen(jnp.broadcast_to(skip_ref[...], (SLOTS, HEADS)), spread)
    inputs, kept = [], []
    for step in range(STEPS):
        step_size = softplus(raws[step])
        kept.append(widen(jnp.exp(-decay_ref[...] * step_size), spread))
        inputs.append(widen(step_size, spread) * xs[step])
    for step in range(STEPS):
        total = read_ref[:, step, :] * kept[0]
        for earlier in range(step + 1):
            if earlier > 0:
                total = total * kept[earlier]
            match = jnp.sum(steps_b[earlier] * steps_c[step], axis=1, keepdims=True)
            total = total + inputs[earlier] * match
        gated = (total + skip * xs[step]) * silu(zs[step])
        scale = lax.rsqrt(jnp.mean(gated * gated, axis=1, keepdims=True) + NORM_EPS)
        rows_ref[step * SLOTS : (step + 1) * SLOTS, :] = gated * scale * gain_ref[...]
    rows = rows_ref[...].astype(BF16)
    wait(11)
    for turn in range(HEADS):
        block = 2 * ((column // 2 + turn) % 4) + (column + turn // 4) % 2
        columns = pl.ds(pl.multiple_of(block * WIDTH, WIDTH), WIDTH)
        terms = contract(rows, weight_ref[:, columns]).astype(BF16)
        if turn < 4:
            keep_ref[turn] = terms
        else:
            send_ref[turn - 4] = terms
    late = kept[2]
    factors = [inputs[0] * (kept[1] * late), inputs[1] * late, inputs[2]]
    outer_ref[...] = jnp.zeros_like(outer_ref)
    kept_ref[...] = jnp.zeros_like(kept_ref)
    b_rows_ref[...] = jnp.zeros_like(b_rows_ref)
    for step in range(STEPS):
        outer_ref[:, step, :] = factors[step]
        b_rows_ref[:, step, :] = steps_b[step]
    kept_ref[:, 0, :] = kept[0] * (kept[1] * late)


def mamba(got, state, *arrays):
    part = shaped((4, ROWS, WIDTH), BF16)
    factor = shaped((SLOTS, 8, WIDTH), F32)
    outs = [part, part, shaped((ROWS, WIDTH), F32), factor, factor, shaped((SLOTS, 8, NSTATE), F32)]
    scratch = [
        pltpu.VMEM((SLOTS, 32, 128), F32),
        pltpu.VMEM((SLOTS, 8, NSTATE), F32),
        pltpu.VMEM((SLOTS, 8, WIDTH), F32),
        pltpu.VMEM((ROWS, WIDTH), F32),
    ]
    args = [(got, "v"), (state, "l")] + [(array, "h") for array in arrays[:-1]] + [(arrays[-1], "l")]
    return run_kernel(mamba_kernel, args, outs, "mamba_steps", scratch, 2 * 24 * 512 * 4096, 8 * 2**20, limit=50)


def update_kernel(ins, outs, scratch, wait):
    table_ref, state_any, outer_ref, keep_ref, b_ref = ins
    (out_any,), (state_ref, made_ref, in_sems, out_sems) = outs, scratch
    first = lax.axis_index("req") * SLOTS
    sources = [table_ref[0, first + block] for block in range(SLOTS)]
    loads = [
        pltpu.make_async_copy(state_any.at[sources[block]], state_ref.at[block], in_sems.at[block])
        for block in range(SLOTS)
    ]
    for load in loads:
        load.start()
    stores = []
    ones = jnp.ones((8, NSTATE), BF16)
    along = ((0,), (0,))
    for block in range(SLOTS):
        b_rows = b_ref[sources[block]].astype(BF16)
        outer_high, outer_low = split_pair(outer_ref[sources[block]])
        keep_high, keep_low = split_pair(keep_ref[sources[block]])
        keep = contract(keep_high, ones, along) + contract(keep_low, ones, along)
        added = contract(outer_high, b_rows, along) + contract(outer_low, b_rows, along)
        loads[block].wait()
        made_ref[block] = (keep * state_ref[block] + added).astype(BF16)
        store = pltpu.make_async_copy(made_ref.at[block], out_any.at[block], out_sems.at[block])
        store.start()
        stores.append(store)
    for store in stores:
        store.wait()


def update_states(table, state, factors):
    scratch = [
        pltpu.VMEM(state.shape, F32),
        pltpu.VMEM(state.shape, BF16),
        pltpu.SemaphoreType.DMA((SLOTS,)),
        pltpu.SemaphoreType.DMA((SLOTS,)),
    ]
    args = [(table, "s"), (state, "m")] + [(factor, "h") for factor in factors]
    return run_kernel(
        update_kernel, args, [shaped(state.shape, BF16)], "update_states", scratch,
        2 * 32 * 512 * 1024, 3 * 2**20, [HBM_SPEC],
    )[0]


CORES = [(i, i ^ 1) for i in range(HEADS)]


LINE = 8
LINES = OWNERS // LINE


def along_x(value, distance):
    moves = [(i, ((i // LINE + distance) % LINES) * LINE + i % LINE) for i in range(OWNERS)]
    return lax.ppermute(value, "req", moves)


def along_y(value, distance):
    moves = [(i, ((i // 2 + distance) % 4) * 2 + i % 2) for i in range(HEADS)]
    return lax.ppermute(value, "head", moves)


def add_kernel(tail, ins, outs, scratch, wait):
    keep_ref, got_ref = ins
    first_ref, *rest_refs = outs
    for turn in range(4):
        total = keep_ref[turn].astype(F32) + got_ref[turn].astype(F32)
        if turn == 0:
            first_ref[...] = total
            continue
        out_ref = rest_refs[turn - 1]
        if tail:
            out_ref[:, : 2 * FFE] = total[:, : 2 * FFE].astype(BF16)
            out_ref[:, 2 * FFE :] = pair_lanes(jnp.sum(total[:, 2 * FFE :], axis=1, keepdims=True))
        else:
            out_ref[...] = total.astype(BF16)


def pair_lanes(value):
    high, low = split_pair(value)
    shape = (value.shape[0], 128)
    lane = iota(shape, 1)
    high_wide = jnp.broadcast_to(high.astype(F32), shape)
    low_wide = jnp.broadcast_to(low.astype(F32), shape)
    return jnp.where(lane == 0, high_wide, jnp.where(lane == 1, low_wide, 0.0)).astype(BF16)


def add_cores(keep, got, tail):
    shape = keep.shape[1:]
    outs = [shaped(shape, F32)] + [shaped(shape, BF16)] * 3
    return run_kernel(
        functools.partial(add_kernel, tail), [(keep, "v"), (got, "v")], outs, "add_cores", moved=4 * keep.size
    )


def scatter_sum(keep, send, tail, beside=None):
    got = lax.ppermute(send, "head", CORES)
    first, *rest = add_cores(keep, got, tail)
    if beside is not None:
        first, beside, *rest = lax.optimization_barrier((first, beside, *rest))
        beside = exchange(beside)
    far = along_y(rest[1], 2)
    near = along_y(rest[0], 1)
    other = along_y(rest[2], 3)
    return (first, near, far, other), beside


def stream_kernel(ins, outs, scratch, wait):
    first_ref, a_ref, b_ref, c_ref, residual_ref = ins
    (out_ref,) = outs
    total = first_ref[...] + a_ref[...].astype(F32) + b_ref[...].astype(F32) + c_ref[...].astype(F32)
    stream = (residual_ref[...] + total).astype(BF16)
    out_ref[...] = jnp.broadcast_to(stream[None], out_ref.shape)


def stream_copies(parts, residual):
    args = [(part, "v") for part in parts] + [(residual, "v")]
    return run_kernel(stream_kernel, args, [shaped((LINE, ROWS, WIDTH), BF16)], "stream_copies")[0]


def routes_kernel(ins, outs, scratch, wait):
    dest_ref, all_ids_ref, ids_ref, weights_ref = ins
    pick_ref, kept_ref, high_ref, low_ref = outs
    me = lax.axis_index("req")
    column = lax.axis_index("head")
    total_rows = OWNERS * ROWS
    square = (REQUESTS, REQUESTS)
    row_id = iota(square, 1)
    col_id = iota(square, 0)
    first = dest_ref[0:1, :]
    second = jnp.broadcast_to(dest_ref[1:2, :], (8, REQUESTS)).astype(F32).astype(BF16)
    hop_one = hot(jnp.broadcast_to(first, square) == col_id)
    both = contract(second, hop_one)[0:1, :].astype(jnp.int32)
    hops = [hot(row_id == col_id), hop_one, hot(jnp.broadcast_to(both, square) == col_id)]
    slots = [iota((1, REQUESTS), 1), first, both]
    spread = []
    for step in range(STEPS):
        shape = (REQUESTS, total_rows)
        g = iota(shape, 0)
        source = (((me >> 3) - (g >> 6)) & 3) * LINE + ((g >> 3) & 7)
        spread.append(hot(iota(shape, 1) == source * ROWS + step * SLOTS + (g & 7)))
    at_row = jnp.zeros((8, total_rows), F32)
    for step in range(STEPS):
        wide = jnp.broadcast_to(slots[step], (8, REQUESTS)).astype(F32).astype(BF16)
        at_row = at_row + contract(wide, spread[step])
    ids = all_ids_ref[...].astype(F32)
    step_of = hot((iota((128, 128), 0) >> 3) == iota((128, 128), 1) + 3)
    earlier = hot(((row_id >> 3) == (col_id >> 3)) & (row_id < col_id))
    slot = iota((REQUESTS, 128), 0)
    lane = iota((REQUESTS, 128), 1)
    owner = slot >> 3
    part = owner >> 2
    turn = (((part & 1) + column) & 1) * 4 + (((part >> 1) - (column >> 1)) & 3)
    base = turn * (CHUNK // 2) + (owner & 3) * (STEPS * CAP) + lane * CAP
    for expert in range(2):
        match = (ids == (me * 2 + expert).astype(F32)) & (lane >= 24) & (lane < 48)
        named = contract(hot(match), step_of)
        rank = contract(earlier, named.astype(BF16))
        target = jnp.where(named > 0.5, base.astype(F32) + rank + 1.0, 0.0).astype(BF16)
        row = jnp.zeros((8, total_rows), F32)
        for step in range(STEPS):
            select = hot(iota((8, 128), 1) == step)
            by_slot = contract(select, target, ((1,), (1,)))
            by_home = contract(by_slot.astype(BF16), hops[step])
            row = row + contract(by_home.astype(BF16), spread[step])
        half = OWNERS * STEPS * CAP
        want = iota((half, total_rows), 0).astype(F32) + 1.0
        pick_ref[expert * half : (expert + 1) * half, :] = hot(jnp.broadcast_to(row[0:1, :], (half, total_rows)) == want)
    shape = (ROWS, total_rows)
    mine = (me * SLOTS + iota(shape, 0) % SLOTS).astype(F32)
    step_match = (iota(shape, 1) % ROWS) // SLOTS == iota(shape, 0) // SLOTS
    kept_ref[...] = hot((jnp.broadcast_to(at_row[0:1, :], shape) == mine) & step_match)
    expert_lane = iota((ROWS, 128), 1)
    chosen = jnp.zeros((ROWS, 128), F32)
    weight = jnp.zeros((ROWS, 128), F32)
    for choice in range(8):
        hit = expert_lane == ids_ref[:, choice : choice + 1]
        chosen = chosen + jnp.where(hit, 1.0, 0.0)
        weight = weight + jnp.where(hit, weights_ref[:, choice : choice + 1], 0.0)
    small = (ROWS, ROWS)
    before = hot((iota(small, 0) // SLOTS == iota(small, 1) // SLOTS) & (iota(small, 1) < iota(small, 0)))
    rank = contract(before, chosen.astype(BF16))
    span = OWNERS * CHUNK
    place = iota((128, span), 1) % CHUNK % 12
    expert_of = 2 * (iota((128, span), 1) // CHUNK) + place // 6
    to_place = hot(iota((128, span), 0) == expert_of)
    spot = iota((ROWS, span), 1) % CHUNK
    fits = (contract(rank.astype(BF16), to_place) == (spot % 2).astype(F32)) & (
        (spot % 6) // 2 == iota((ROWS, span), 0) // SLOTS
    )
    for value, out_ref in zip(split_pair(weight), (high_ref, low_ref)):
        out_ref[...] = jnp.where(fits, contract(value, to_place), 0.0).astype(BF16)


def routes(dest, all_ids, ids, weights):
    total_rows = OWNERS * ROWS
    mixing = shaped((ROWS, OWNERS * CHUNK), BF16)
    outs = [
        shaped((2 * OWNERS * STEPS * CAP, total_rows), BF16),
        shaped((ROWS, total_rows), BF16),
        mixing,
        mixing,
    ]
    args = [(dest, "h"), (all_ids, "v"), (ids, "h"), (weights, "h")]
    return run_kernel(routes_kernel, args, outs, "routes", flops=10**9)


def expand_kernel(ins, outs, scratch, wait):
    pick_ref, kept_ref, *stream_refs, gain_ref, gate_ref, up_ref = ins
    keep_ref, send_ref, own_ref = outs

    def choose(rows):
        total = 0.0
        for line, ref in enumerate(stream_refs):
            total = total + contract(rows[:, line * LINE * ROWS : (line + 1) * LINE * ROWS], ref[...])
        return total

    own_ref[...] = choose(kept_ref[...]).astype(BF16)
    half = pick_ref.shape[0] // 2
    some = CHUNK // 2
    for expert in range(2):
        picked = choose(pick_ref[expert * half : (expert + 1) * half, :])
        tail = pair_lanes(jnp.sum(picked * picked, axis=1, keepdims=True))
        scaled = (picked * gain_ref[...]).astype(BF16)
        if expert == 0:
            wait(7)
            wait(8)
        values = [
            contract(scaled, gate_ref[expert]).astype(BF16),
            contract(scaled, up_ref[expert]).astype(BF16),
            tail,
        ]
        rows = slice(expert * some, (expert + 1) * some)
        for turn in range(HEADS):
            out_ref = keep_ref if turn < 4 else send_ref
            source = slice(turn * some, (turn + 1) * some)
            for value, start in zip(values, (0, FFE, 2 * FFE)):
                out_ref[turn % 4, rows, start : start + value.shape[1]] = value[source, :]


def expand(pick, kept, streams, gain, gate_weight, up_weight):
    part = shaped((4, CHUNK, TERMS), BF16)
    args = [(pick, "h"), (kept, "h")] + [(stream, "v") for stream in streams]
    args += [(gain, "h"), (gate_weight, "l"), (up_weight, "l")]
    return run_kernel(
        expand_kernel, args, [part, part, shaped((ROWS, WIDTH), BF16)], "expand_experts", flops=2 * 384 * 512 * (2048 + 768), moved=8 * 2**20
    )


def hidden_kernel(ins, outs, scratch, wait):
    first_ref, a_ref, b_ref, c_ref = ins
    (out_ref,) = outs
    total = first_ref[...] + a_ref[...].astype(F32) + b_ref[...].astype(F32) + c_ref[...].astype(F32)
    square = jnp.sum(total[:, 2 * FFE :], axis=1, keepdims=True)
    inverse = lax.rsqrt(square * (1.0 / (HEADS * WIDTH)) + NORM_EPS)
    out_ref[...] = (silu(total[:, :FFE] * inverse) * (total[:, FFE : 2 * FFE] * inverse)).astype(BF16)


def hidden_units(parts):
    args = [(part, "v") for part in parts]
    return run_kernel(hidden_kernel, args, [shaped((CHUNK, FFE), BF16)], "hidden_units")[0]


def shrink_kernel(ins, outs, scratch, wait):
    table_ref, pieces_ref, weight_ref, *hidden_refs = ins
    (out_ref,), (sems,) = outs, scratch
    first = lax.axis_index("req") // 4 * OWNERS
    column = lax.axis_index("head")
    moves = [
        pltpu.make_async_copy(
            pieces_ref.at[table_ref[1, first + block]],
            out_ref.at[block, pl.ds(CHUNK, 2 * HSIZE), :],
            sems.at[block],
        )
        for block in range(OWNERS)
    ]
    for move in moves:
        move.start()
    hidden = jnp.concatenate([ref[...] for ref in hidden_refs], axis=0)
    wait(2)
    served = [contract(hidden, weight_ref[expert]) for expert in range(2)]
    shape = (4 * 16, CHUNK)
    row, source = iota(shape, 0), iota(shape, 1)
    inside = row % 16
    spot = hot((inside < 12) & (source == (inside // 6) * (CHUNK // 2) + (row // 16) * 6 + inside % 6))
    half = iota((CHUNK, WIDTH), 0) < CHUNK // 2
    for turn in range(HEADS):
        rows = slice(turn * CHUNK, (turn + 1) * CHUNK)
        chunk = jnp.where(half, served[0][rows], served[1][rows]).astype(BF16)
        owner = (2 * ((column // 2 - turn + 8) % 4) + (column + turn // 4) % 2) * 4
        block = contract(spot, chunk)
        for piece in range(4):
            wide = block[piece * 16 : piece * 16 + 12, :]
            cut = [wide[:, 128 * i : 128 * (i + 1)] for i in range(4)]
            out_ref[owner + piece, 0:CHUNK, :] = jnp.concatenate(cut, axis=0).astype(BF16)
    for move in moves:
        move.wait()


def shrink(table, pieces, hidden, weight):
    args = [(table, "s"), (pieces, "m"), (weight, "l")] + [(block, "v") for block in hidden]
    outs = [shaped((OWNERS, CHUNK + 2 * HSIZE, 128), BF16)]
    return run_kernel(
        shrink_kernel, args, outs, "shrink_experts", [pltpu.SemaphoreType.DMA((OWNERS,))],
        2 * 2 * 384 * 1024 * 512, 4 * 2**20, limit=56,
    )[0]


def finish_kernel(ins, outs, scratch, wait):
    table_ref, back_ref, high_ref, low_ref, stream_ref = ins
    mixed_ref, states_any = outs
    made_ref, sems = scratch
    first = lax.axis_index("req") * SLOTS
    stores = []
    for slot in range(SLOTS):
        color = table_ref[2, first + slot]
        for piece in range(4):
            rows = slice(piece * 2 * HSIZE, (piece + 1) * 2 * HSIZE)
            made_ref[slot, rows, :] = back_ref[color * 4 + piece, CHUNK:, :].astype(F32)
        store = pltpu.make_async_copy(made_ref.at[slot], states_any.at[slot], sems.at[slot])
        store.start()
        stores.append(store)
    served = back_ref[:, 0:CHUNK, :].reshape(OWNERS * CHUNK, 128)
    for ref in (2, 3, 4):
        wait(ref)
    stream = stream_ref[...].astype(F32)
    high, low = high_ref[...].astype(F32), low_ref[...].astype(F32)
    for piece in range(4):
        columns = slice(piece * 128, (piece + 1) * 128)
        here = iota((ROWS, OWNERS * CHUNK), 1) % CHUNK // 12 == piece
        mixed = contract(jnp.where(here, high, 0.0).astype(BF16), served)
        mixed = mixed + contract(jnp.where(here, low, 0.0).astype(BF16), served)
        mixed_ref[:, columns] = (stream[:, columns] + mixed).astype(BF16)
    for store in stores:
        store.wait()


def finish(table, back, high, low, stream):
    args = [(table, "s"), (back, "v"), (high, "l"), (low, "l"), (stream, "l")]
    outs = [shaped((ROWS, WIDTH), BF16), shaped((SLOTS, HEADS * HSIZE, NSTATE), F32)]
    scratch = [pltpu.VMEM((SLOTS, HEADS * HSIZE, NSTATE), F32), pltpu.SemaphoreType.DMA((SLOTS,))]
    return run_kernel(
        finish_kernel, args, outs, "finish", scratch, 10**8, 4 * 2**20, [VMEM_SPEC, HBM_SPEC]
    )


def exchange(value):
    return lax.all_to_all(value, "req", split_axis=0, concat_axis=0, tiled=True)


def shards(
    states, ssm_x, gate_z, ssm_b, ssm_c, dt_raw, decay_rate, skip_gain, ssm_gain, out_weight,
    residual, ffn_gain, route_ids, route_weights, gate_weight, up_weight, down_weight, dest,
):
    fence = lax.optimization_barrier
    state_rows = states.reshape(SLOTS, HEADS * HSIZE, NSTATE)
    own = (ssm_x, gate_z, residual, ssm_b, ssm_c, dt_raw)

    message, most = pack_few(dest, *own, route_ids)

    def few(message):
        scratch = [pltpu.VMEM((OWNERS, SLOTS, 128), F32)]
        got, table = fence((exchange(message), routing_tables(dest)))
        return take(take_few_kernel, dest, got, scratch) + (table,)

    def every(_):
        scratch = [pltpu.VMEM((SLOTS, MESSAGE, 128), F32), pltpu.VMEM((SLOTS, 16, 128), F32)]
        got, table = fence((exchange(pack_all(dest, *own, route_ids)), routing_tables(dest)))
        return take(take_all_kernel, dest, got, scratch) + (table,)

    rows, all_ids, table = lax.cond(most[0, 0] <= SPARE, few, every, message)

    keep_part, send_part, home_residual, *factors = mamba(
        rows, state_rows, *own, decay_rate[None], skip_gain[None], ssm_gain[None], out_weight
    )
    parts, _ = scatter_sum(keep_part, send_part, False)
    copies, later_dest, all_ids, factors = fence((stream_copies(parts, home_residual), dest, all_ids, factors))
    lines = [[line * LINE + place for place in range(LINE)] for line in range(LINES)]
    line = lax.all_to_all(
        copies, "req", split_axis=0, concat_axis=0, axis_index_groups=lines, tiled=True
    ).reshape(LINE * ROWS, WIDTH)
    pieces = update_states(table, state_rows, factors)
    routed = routes(later_dest, all_ids, route_ids.reshape(ROWS, 8), route_weights.reshape(ROWS, 8))
    line, pieces, (pick, kept, high, low) = fence((line, pieces, routed))
    streams = [line, along_x(line, 1), along_x(line, 2), along_x(line, 3)]
    streams[1], pieces = fence((streams[1], pieces))
    pieces = exchange(pieces.reshape(OWNERS, 2 * HSIZE, NSTATE))

    keep_part, send_part, own_stream = expand(pick, kept, streams, ffn_gain[None], gate_weight, up_weight)
    parts, _ = scatter_sum(keep_part, send_part, True)
    hidden = hidden_units(parts)
    far = along_y(hidden, 2)
    near = along_y(hidden, 1)
    other = along_y(hidden, 3)
    blocks = [hidden, near, far, other]
    blocks = blocks + [lax.ppermute(block, "head", CORES) for block in blocks]
    back = exchange(shrink(table, pieces, blocks, down_weight))
    mixed, final_states = finish(table, back, high, low, own_stream)
    return mixed.reshape(STEPS, SLOTS, WIDTH), final_states.reshape(states.shape)


def solution(mesh):
    placed = (
        P("req", "head", None, None),
        P(None, "req", "head"),
        P(None, "req", "head"),
        P(None, "req", "head"),
        P(None, "req", "head"),
        P(None, "req", "head"),
        P("head"),
        P("head"),
        P("head"),
        P("head", None),
        P(None, "req", None),
        P("head"),
        P(None, "req", None),
        P(None, "req", None),
        P("req", "head", None),
        P("req", "head", None),
        P("req", None, "head"),
        P(),
    )
    return jax.shard_map(
        shards,
        mesh=mesh,
        in_specs=placed,
        out_specs=(P(None, "req", "head"), P("req", "head", None, None)),
        check_vma=False,
    )
```
